128 devices in a mesh: seq: 16 (over z, x_lo, core), head: 8 (over y, x_hi).
Axes of the slice: x: 4 (x_hi: 2, x_lo: 2; x = x_hi * 2 + x_lo), y: 4, z: 4, core: 2. Of those that a mesh axis runs over, the one named last changes fastest.
Arguments:
- teacher: bfloat16 [2048, 3, 8192], P('seq', None, 'head')
- student: bfloat16 [2048, 3, 4096], P('seq', None, 'head')
- table: int32 [64], replicated, may hold values from 0 to 63, each once
Outputs:
- loss: float32 [], replicated
- grads: bfloat16 [2048, 3, 4096], P('seq', None, 'head')
The draws below stay inside these ranges and needn't reach their ends.
Inputs may be any that keep to these rules, and one draw needn't show every extreme that they name: `table`: each teacher head stands in exactly one slot.
All inputs are finite; a program needn't handle non-finite values.
Results may differ from the reference program's by a relative error of at most 0.0055.
Values may be sent and summed in bfloat16 or wider, within the bound.
A program may use at most 128 MiB of HBM per device.

```python
import math
import jax
import jax.numpy as jnp
from jax import lax

TOK_DEV = 128
HD = 128
RH = 32
GRP = 2
TH = 64
DT = 8192
DS = 4096
LEN = 2048
N_SEQ = 16


def draw_teacher(key, part):
    key = jax.random.fold_in(key, 11)
    key_one = jax.random.fold_in(key, 0)
    values = 0.5 * jax.random.normal(key_one, (LEN, 3, DT), jnp.float32)
    return values.astype(jnp.bfloat16)


def draw_student(key, part):
    key = jax.random.fold_in(key, 23)
    key_one = jax.random.fold_in(key, 0)
    values = 0.5 * jax.random.normal(key_one, (LEN, 3, DS), jnp.float32)
    return values.astype(jnp.bfloat16)


def setup_inputs(seed: int = 0) -> dict:
    keys = jax.random.split(jax.random.key(seed), 4)
    teacher = draw_teacher(jax.random.fold_in(keys[3], 71), 0)
    student = draw_student(jax.random.fold_in(keys[3], 71), 0)
    table = jax.random.permutation(keys[2], TH).astype(jnp.int32)
    return {"teacher": teacher, "student": student, "table": table}


def reference(teacher, student, table):
    heads = teacher.reshape(LEN, 3, TH, HD)
    rel_teacher = jnp.take(heads, table, axis=2).reshape(LEN, 3, RH, GRP * HD)
    rel_student = student.reshape(LEN, 3, RH, HD)
    teach_full = rel_teacher.astype(jnp.float32)
    stud_full = rel_student.astype(jnp.float32)
    scale_teach = 1.0 / math.sqrt(GRP * HD)
    scale_stud = 1.0 / math.sqrt(HD)
    key_pos = jnp.arange(LEN, dtype=jnp.int32)

    def query_block(col_grad, block_index):
        first_row = (block_index * TOK_DEV).astype(jnp.int32)
        query_teach = lax.dynamic_slice_in_dim(teach_full, first_row, TOK_DEV, 0)
        query_stud = lax.dynamic_slice_in_dim(stud_full, first_row, TOK_DEV, 0)
        positions = first_row + jnp.arange(TOK_DEV, dtype=jnp.int32)
        allowed = key_pos[None, :] <= positions[:, None]
        teach_logit = jnp.einsum('qahd,kahd->ahqk', query_teach, teach_full) * scale_teach
        stud_logit = jnp.einsum('qahd,kahd->ahqk', query_stud, stud_full) * scale_stud
        teach_logit = jnp.where(allowed, teach_logit, -1e+30)
        stud_logit = jnp.where(allowed, stud_logit, -1e+30)
        top_teach = lax.optimization_barrier(jnp.max(teach_logit, axis=-1, keepdims=True))
        lse_teach = top_teach + jnp.log(lax.optimization_barrier(jnp.sum(jnp.exp(teach_logit - top_teach), axis=-1, keepdims=True)))
        top_stud = lax.optimization_barrier(jnp.max(stud_logit, axis=-1, keepdims=True))
        lse_stud = top_stud + jnp.log(lax.optimization_barrier(jnp.sum(jnp.exp(stud_logit - top_stud), axis=-1, keepdims=True)))
        teach_prob = jnp.where(allowed, jnp.exp(teach_logit - lse_teach), 0.0)
        stud_prob = jnp.where(allowed, jnp.exp(stud_logit - lse_stud), 0.0)
        diverge = jnp.where(allowed, teach_prob * (teach_logit - lse_teach - (stud_logit - lse_stud)), 0.0)
        kl_part = jnp.sum(diverge)
        diff_low = lax.optimization_barrier((stud_prob - teach_prob).astype(jnp.bfloat16))
        diff = diff_low.astype(jnp.float32)
        row_grad = jnp.einsum('ahqk,kahd->qahd', diff, stud_full)
        col_grad = col_grad + jnp.einsum('ahqk,qahd->kahd', diff, query_stud)
        return (col_grad, (row_grad, kl_part))
    start_col = jnp.zeros((LEN, 3, RH, HD), jnp.float32)
    col_grad, (row_blocks, kl_parts) = lax.scan(query_block, start_col, jnp.arange(N_SEQ, dtype=jnp.int32))
    row_grad = row_blocks.reshape(LEN, 3, RH, HD)
    grads = ((row_grad + col_grad) * scale_stud).reshape(LEN, 3, DS).astype(jnp.bfloat16)
    loss = jnp.sum(kl_parts) / (3.0 * RH * LEN)
    return (loss, grads)
```

```python
import functools
import math

import jax
import jax.numpy as jnp
from jax import lax
from jax.experimental import pallas as pl
from jax.experimental.pallas import tpu as pltpu
from jax.sharding import PartitionSpec as P

HD = 128
GRP = 2
BLK = 256
NEG = -1e30
MESH = pl.DeviceIdType.MESH
F32 = jnp.float32
BF16 = jnp.bfloat16
LOG2E = math.log2(math.e)


def owner_seq(p, rl):
    return 4 * rl + lax.rem(p + rl + 1, 4)


def owner_of_static(s):
    rl = s // 4
    p = (s % 4 - rl - 1) % 4
    return p, rl


def await_bytes(ref, sem):
    pltpu.make_async_copy(ref, ref, sem).wait()


def dot_t(a, b):
    return lax.dot_general(a, b, (((1,), (1,)), ((), ())), preferred_element_type=F32)


def kernel(
    ns, nh, table, teacher, student, loss, grads,
    got0, got1, got2, flat0, flat1, flat2, stage0, stage1, stage2,
    t_all, s_all, s_turn, log_s, prob_s, work, col, back, l_mine, l_seq, l_head,
    p1_send, p1_recv, s_send, s_recv, p2_send, t_recv, g_send, g_recv, l_send, l_recv,
):
    rows = teacher.shape[1]
    width = teacher.shape[2]
    slots = width // HD
    sub = rows // nh
    rels = student.shape[2] // HD
    rel_all = rels * nh
    tokens = rows * ns
    blocks = tokens // BLK
    per_blk = BLK // rows
    me_s = lax.axis_index("seq")
    me_g = lax.axis_index("head")
    my_rl = me_s // 4
    my_p = lax.rem(lax.rem(me_s, 4) - my_rl + 7, 4)
    active = my_p < 3
    got = (got0, got1, got2)
    flat = (flat0, flat1, flat2)
    stage = (stage0, stage1, stage2)

    def send(src, dst, ssem, rsem, s, g):
        pltpu.make_async_remote_copy(
            src_ref=src, dst_ref=dst, send_sem=ssem, recv_sem=rsem,
            device_id=(s, g), device_id_type=MESH,
        ).start()

    for p in range(3):
        for step in range(1, nh):
            g = lax.rem(me_g + step, nh)
            send(
                teacher.at[p, pl.ds(g * sub, sub), :], got[p].at[me_g],
                p1_send, p1_recv.at[p], me_s, g,
            )
        pltpu.make_async_copy(
            teacher.at[p, pl.ds(me_g * sub, sub), :], got[p].at[me_g], p1_recv.at[p]
        ).start()

    def student_out(i, c):
        q = lax.rem(i + me_s, 3 * rels)
        p = q // rels
        rl = lax.rem(q, rels)
        s = owner_seq(p, rl)
        src = student.at[p, :, pl.ds(pl.multiple_of(rl * HD, HD), HD)]
        dst = s_all.at[pl.ds(pl.multiple_of(me_s * rows, rows), rows), :]

        @pl.when(s != me_s)
        def _():
            send(src, dst, s_send, s_recv, s, me_g)

        @pl.when(s == me_s)
        def _():
            pltpu.make_async_copy(src, dst, s_recv).start()

        return c

    lax.fori_loop(0, 3 * rels, student_out, 0)

    for p in range(3):
        await_bytes(got[p], p1_recv.at[p])
        for h in range(slots * nh):
            lane = h % slots * HD
            flat[p][h] = got[p][h // slots, :, lane : lane + HD]

        def relation_out(i, c):
            r = lax.rem(i + 2 * me_s + rels * me_g, rel_all)
            for k in range(GRP):
                stage[p][r, :, k * HD : (k + 1) * HD] = flat[p][table[GRP * r + k]]
            g = r // rels
            s = owner_seq(p, lax.rem(r, rels))
            src = stage[p].at[r]
            dst = t_all.at[pl.ds(pl.multiple_of(me_s * rows + me_g * sub, sub), sub), :]
            here = jnp.logical_and(s == me_s, g == me_g)

            @pl.when(jnp.logical_not(here))
            def _():
                send(src, dst, p2_send, t_recv, s, g)

            @pl.when(here)
            def _():
                pltpu.make_async_copy(src, dst, t_recv).start()

            return c

        lax.fori_loop(0, rel_all, relation_out, 0)

    scale_t = LOG2E / math.sqrt(GRP * HD)
    scale_s = LOG2E / math.sqrt(HD)
    key_row = lax.broadcasted_iota(jnp.int32, (BLK, BLK), 0)
    query_col = lax.broadcasted_iota(jnp.int32, (BLK, BLK), 1)

    def at_block(b):
        return pl.ds(pl.multiple_of(b * BLK, BLK), BLK)

    def fold(op, x):
        return op(x.reshape(BLK // 8, 8, BLK), axis=0)

    @pl.when(active)
    def _():
        await_bytes(s_all, s_recv)

        def turn(b, c):
            s_turn[:, at_block(b)] = s_all[at_block(b), :].T
            col[at_block(b), :] = jnp.zeros((BLK, HD), F32)
            return c

        lax.fori_loop(0, blocks, turn, 0)

        def student_block(qb, c):
            base = qb * (qb + 1) // 2
            query = s_all[at_block(qb), :]

            def first(kb, top):
                logit = dot_t(s_all[at_block(kb), :], query) * scale_s
                log_s[base + kb] = logit
                return jnp.maximum(top, fold(jnp.max, logit))

            top = lax.fori_loop(0, qb, first, jnp.full((8, BLK), NEG, F32))
            logit = jnp.where(key_row <= query_col, dot_t(query, query) * scale_s, NEG)
            log_s[base + qb] = logit
            top = jnp.max(jnp.maximum(top, fold(jnp.max, logit)), axis=0, keepdims=True)

            def second(kb, total):
                weight = jnp.exp2(log_s[base + kb] - top)
                prob_s[base + kb] = weight
                return total + fold(jnp.sum, weight)

            total = lax.fori_loop(0, qb + 1, second, jnp.zeros((8, BLK), F32))
            total = jnp.sum(total, axis=0, keepdims=True)
            inverse = 1.0 / total
            lse = top + jnp.log2(total)

            def third(kb, c):
                log_s[base + kb] = log_s[base + kb] - lse
                prob_s[base + kb] = prob_s[base + kb] * inverse
                return c

            lax.fori_loop(0, qb + 1, third, 0)
            return c

        lax.fori_loop(0, blocks, student_block, 0)

        await_bytes(t_all, t_recv)

        def teacher_block(i, loss_row):
            qb = blocks - 1 - i
            base = qb * (qb + 1) // 2
            query = t_all[at_block(qb), :]

            def first(kb, top):
                logit = dot_t(t_all[at_block(kb), :], query) * scale_t
                work[kb] = logit
                return jnp.maximum(top, fold(jnp.max, logit))

            top = lax.fori_loop(0, qb, first, jnp.full((8, BLK), NEG, F32))
            logit = jnp.where(key_row <= query_col, dot_t(query, query) * scale_t, NEG)
            work[qb] = logit
            top = jnp.max(jnp.maximum(top, fold(jnp.max, logit)), axis=0, keepdims=True)

            def second(kb, carried):
                total, cross = carried
                shifted = work[kb] - top
                weight = jnp.exp2(shifted)
                work[kb] = weight
                return (
                    total + fold(jnp.sum, weight),
                    cross + fold(jnp.sum, weight * (shifted - log_s[base + kb])),
                )

            zero = jnp.zeros((8, BLK), F32)
            total, cross = lax.fori_loop(0, qb + 1, second, (zero, zero))
            total = jnp.sum(total, axis=0, keepdims=True)
            cross = jnp.sum(cross, axis=0, keepdims=True)
            inverse = 1.0 / total
            query_s = s_all[at_block(qb), :]

            def third(kb, row):
                diff = (prob_s[base + kb] - work[kb] * inverse).astype(BF16)
                col[at_block(kb), :] += jnp.dot(diff, query_s, preferred_element_type=F32)
                return row + jnp.dot(s_turn[:, at_block(kb)], diff, preferred_element_type=F32)

            row = lax.fori_loop(0, qb + 1, third, jnp.zeros((HD, BLK), F32))
            block = (col[at_block(qb), :] + row.T) * (1.0 / math.sqrt(HD))
            back[at_block(qb), :] = block.astype(BF16)
            for j in range(per_blk):
                s = qb * per_blk + j
                src = back.at[pl.ds(pl.multiple_of(s * rows, rows), rows), :]
                dst = grads.at[my_p, :, pl.ds(pl.multiple_of(my_rl * HD, HD), HD)]

                @pl.when(s != me_s)
                def _():
                    send(src, dst, g_send, g_recv, s, me_g)

                @pl.when(s == me_s)
                def _():
                    pltpu.make_async_copy(src, dst, g_recv).start()

            return loss_row + (cross * inverse - jnp.log2(total))

        loss_row = lax.fori_loop(0, blocks, teacher_block, jnp.zeros((1, BLK), F32))
        mine = jnp.full((8, HD), jnp.sum(loss_row), F32)
        l_mine[...] = mine
        l_seq[me_s] = mine

        def loss_out(i, c):
            s = lax.rem(me_s + 1 + i, ns)
            send(l_mine, l_seq.at[me_s], l_send.at[0], l_recv.at[0], s, me_g)
            return c

        lax.fori_loop(0, ns - 1, loss_out, 0)
        await_bytes(l_seq.at[pl.ds(0, 3 * rels - 1)], l_recv.at[0])

    @pl.when(jnp.logical_not(active))
    def _():
        await_bytes(l_seq.at[pl.ds(0, 3 * rels)], l_recv.at[0])

    group = jnp.zeros((8, HD), F32)
    for s in range(ns):
        if owner_of_static(s)[0] < 3:
            group = group + l_seq[s]
    l_head[me_g] = group
    for step in range(1, nh):
        send(l_head.at[me_g], l_head.at[me_g], l_send.at[1], l_recv.at[1], me_s, lax.rem(me_g + step, nh))
    await_bytes(l_head.at[pl.ds(0, nh - 1)], l_recv.at[1])
    total = l_head[0]
    for g in range(1, nh):
        total = total + l_head[g]
    loss[0] = total[0, 0] * (1.0 / (LOG2E * 3.0 * rel_all * tokens))

    await_bytes(grads, g_recv)
    await_bytes(teacher.at[:, pl.ds(0, rows - sub), :], p1_send)

    @pl.when(active)
    def _():
        await_bytes(back.at[pl.ds(0, (3 * rels - 1) * rows), :], s_send)
        await_bytes(back.at[pl.ds(0, (ns - 1) * rows), :], g_send)
        await_bytes(t_all.at[pl.ds(0, (3 * rel_all - 1) * sub), :], p2_send)
        await_bytes(l_seq.at[pl.ds(0, ns - 1)], l_send.at[0])

    @pl.when(jnp.logical_not(active))
    def _():
        await_bytes(back.at[pl.ds(0, 3 * rels * rows), :], s_send)
        await_bytes(t_all.at[pl.ds(0, 3 * rel_all * sub), :], p2_send)

    await_bytes(l_head.at[pl.ds(0, nh - 1)], l_send.at[1])


def solution(mesh):
    ns = mesh.shape["seq"]
    nh = mesh.shape["head"]

    def body(teacher, student, table):
        rows, _, width = teacher.shape
        swidth = student.shape[2]
        sub = rows // nh
        rel_all = swidth // HD * nh
        tokens = rows * ns
        blocks = tokens // BLK
        tiles = blocks * (blocks + 1) // 2
        dma = pltpu.SemaphoreType.DMA
        loss, grads = pl.pallas_call(
            functools.partial(kernel, ns, nh),
            out_shape=(
                jax.ShapeDtypeStruct((1,), F32),
                jax.ShapeDtypeStruct((3, rows, swidth), BF16),
            ),
            in_specs=[
                pl.BlockSpec(memory_space=pltpu.SMEM),
                pl.BlockSpec(memory_space=pl.ANY),
                pl.BlockSpec(memory_space=pl.ANY),
            ],
            out_specs=(
                pl.BlockSpec(memory_space=pltpu.SMEM),
                pl.BlockSpec(memory_space=pl.ANY),
            ),
            scratch_shapes=[pltpu.VMEM((nh, sub, width), BF16)] * 3
            + [pltpu.VMEM((width // HD * nh, sub, HD), BF16)] * 3
            + [pltpu.VMEM((rel_all, sub, GRP * HD), BF16)] * 3
            + [
                pltpu.VMEM((tokens, GRP * HD), BF16),
                pltpu.VMEM((tokens, HD), BF16),
                pltpu.VMEM((HD, tokens), BF16),
                pltpu.VMEM((tiles, BLK, BLK), F32),
                pltpu.VMEM((tiles, BLK, BLK), F32),
                pltpu.VMEM((blocks, BLK, BLK), F32),
                pltpu.VMEM((tokens, HD), F32),
                pltpu.VMEM((tokens, HD), BF16),
                pltpu.VMEM((8, HD), F32),
                pltpu.VMEM((ns, 8, HD), F32),
                pltpu.VMEM((nh, 8, HD), F32),
                dma, dma((3,)), dma, dma, dma, dma, dma, dma, dma((2,)), dma((2,)),
            ],
            compiler_params=pltpu.CompilerParams(
                has_side_effects=True, vmem_limit_bytes=48 * 1024 * 1024
            ),
            cost_estimate=pl.CostEstimate(
                flops=tokens * tokens * 1280, bytes_accessed=4 * 1024 * 1024,
                transcendentals=tokens * tokens,
            ),
            name="relations",
        )(table, jnp.transpose(teacher, (1, 0, 2)), jnp.transpose(student, (1, 0, 2)))
        return loss.reshape(()), jnp.transpose(grads, (1, 0, 2))

    return jax.shard_map(
        body,
        mesh=mesh,
        in_specs=(P("seq", None, "head"), P("seq", None, "head"), P()),
        out_specs=(P(), P("seq", None, "head")),
        check_vma=False,
    )
```

```python
import functools
import math

import jax
import jax.numpy as jnp
from jax import lax
from jax.experimental import pallas as pl
from jax.experimental.pallas import tpu as pltpu
from jax.sharding import PartitionSpec as P

HD = 128
GRP = 2
BLK = 256
NEG = -1e30
MESH = pl.DeviceIdType.MESH
F32 = jnp.float32
BF16 = jnp.bfloat16
LOG2E = math.log2(math.e)


def owner_seq(p, rl):
    return 4 * rl + lax.rem(p + rl + 1, 4)


def owner_of_static(s):
    rl = s // 4
    p = (s % 4 - rl - 1) % 4
    return p, rl


def await_bytes(ref, sem):
    pltpu.make_async_copy(ref, ref, sem).wait()


def dot_t(a, b):
    return lax.dot_general(a, b, (((1,), (1,)), ((), ())), preferred_element_type=F32)


def kernel(
    ns, nh, table_hbm, teacher, student, loss, grads, table,
    got0, got1, got2, flat0, flat1, flat2, stage0, stage1, stage2,
    t_all, s_all, s_turn, log_s, w_s, w_t, top_s, top_t, lse_s, lse_t, col, back,
    l_mine, l_seq, l_head,
    tab_sem, p1_send, p1_recv, s_send, s_recv, p2_send, t_recv, g_send, g_recv, l_send, l_recv, all_in,
):
    rows = teacher.shape[1]
    width = teacher.shape[2]
    slots = width // HD
    sub = rows // nh
    rels = student.shape[2] // HD
    rel_all = rels * nh
    tokens = rows * ns
    wide = tokens // (2 * BLK)
    per_blk = 2 * BLK // rows
    me_s = lax.axis_index("seq")
    me_g = lax.axis_index("head")
    my_rl = me_s // 4
    my_p = lax.rem(lax.rem(me_s, 4) - my_rl + 7, 4)
    active = my_p < 3
    got = (got0, got1, got2)
    flat = (flat0, flat1, flat2)
    stage = (stage0, stage1, stage2)

    def send(src, dst, ssem, rsem, s, g):
        pltpu.make_async_remote_copy(
            src_ref=src, dst_ref=dst, send_sem=ssem, recv_sem=rsem,
            device_id=(s, g), device_id_type=MESH,
        ).start()

    barrier = pltpu.get_barrier_semaphore()

    def greet(sem, along_seq):
        def one(i, c):
            if along_seq:
                to = (lax.rem(me_s + i, ns), me_g)
            else:
                to = (me_s, lax.rem(me_g + i, nh))
            pl.semaphore_signal(sem, inc=1, device_id=to, device_id_type=MESH)
            return c

        lax.fori_loop(1, ns if along_seq else nh, one, 0)

    greet(barrier, False)
    greet(barrier, True)
    table_copy = pltpu.make_async_copy(table_hbm, table, tab_sem)
    table_copy.start()
    pl.semaphore_wait(barrier, ns + nh - 2)

    for p in range(3):
        for step in range(1, nh):
            g = lax.rem(me_g + step, nh)
            send(
                teacher.at[p, pl.ds(g * sub, sub), :], got[p].at[me_g],
                p1_send, p1_recv.at[p], me_s, g,
            )
        pltpu.make_async_copy(
            teacher.at[p, pl.ds(me_g * sub, sub), :], got[p].at[me_g], p1_recv.at[p]
        ).start()

    greet(all_in, False)

    def student_out(i, c):
        q = lax.rem(i + me_s, 3 * rels)
        p = q // rels
        rl = lax.rem(q, rels)
        s = owner_seq(p, rl)
        src = student.at[p, :, pl.ds(pl.multiple_of(rl * HD, HD), HD)]
        dst = s_all.at[pl.ds(pl.multiple_of(me_s * rows, rows), rows), :]

        @pl.when(s != me_s)
        def _():
            send(src, dst, s_send, s_recv, s, me_g)

        @pl.when(s == me_s)
        def _():
            pltpu.make_async_copy(src, dst, s_recv).start()

        return c

    lax.fori_loop(0, 3 * rels, student_out, 0)
    table_copy.wait()
    pl.semaphore_wait(all_in, nh - 1)

    for p in range(3):
        await_bytes(got[p], p1_recv.at[p])
        for h in range(slots * nh):
            lane = h % slots * HD
            flat[p][h] = got[p][h // slots, :, lane : lane + HD]

        def relation_out(i, c):
            r = lax.rem(i + 2 * me_s + rels * me_g, rel_all)
            for k in range(GRP):
                stage[p][r, :, k * HD : (k + 1) * HD] = flat[p][table[GRP * r + k]]
            g = r // rels
            s = owner_seq(p, lax.rem(r, rels))
            src = stage[p].at[r]
            dst = t_all.at[pl.ds(pl.multiple_of(me_s * rows + me_g * sub, sub), sub), :]
            here = jnp.logical_and(s == me_s, g == me_g)

            @pl.when(jnp.logical_not(here))
            def _():
                send(src, dst, p2_send, t_recv, s, g)

            @pl.when(here)
            def _():
                pltpu.make_async_copy(src, dst, t_recv).start()

            return c

        lax.fori_loop(0, rel_all, relation_out, 0)

    scale_t = LOG2E / math.sqrt(GRP * HD)
    scale_s = LOG2E / math.sqrt(HD)
    key_row = lax.broadcasted_iota(jnp.int32, (BLK, BLK), 0)
    query_col = lax.broadcasted_iota(jnp.int32, (BLK, BLK), 1)
    deep = (BLK // 8, 8, BLK)

    def at_block(b):
        return pl.ds(pl.multiple_of(b * BLK, BLK), BLK)

    def tile_of(kb, qb):
        return qb * (qb + 1) // 2 + kb

    def logits(feats, kb, query, scale, diagonal):
        out = dot_t(feats[at_block(kb), :], query) * scale
        if diagonal:
            out = jnp.where(key_row <= query_col, out, NEG)
        return out.reshape(deep)

    def student_tile(kb, qb, query, state, diagonal):
        top, total = state
        t = tile_of(kb, qb)
        logit = logits(s_all, kb, query, scale_s, diagonal)
        new = jnp.maximum(top, jnp.max(logit, axis=0))
        weight = jnp.exp2(logit - new)
        log_s[t] = logit.reshape(BLK, BLK)
        w_s[t] = weight.reshape(BLK, BLK)
        top_s[t] = new
        return new, total * jnp.exp2(top - new) + jnp.sum(weight, axis=0)

    def teacher_tile(kb, qb, query, state, diagonal):
        top, total, cross = state
        t = tile_of(kb, qb)
        logit = logits(t_all, kb, query, scale_t, diagonal)
        new = jnp.maximum(top, jnp.max(logit, axis=0))
        weight = jnp.exp2(logit - new)
        w_t[t] = weight.reshape(BLK, BLK)
        top_t[t] = new
        again = jnp.exp2(top - new)
        gap = logit - log_s[t].reshape(deep)
        return (
            new,
            total * again + jnp.sum(weight, axis=0),
            cross * again + jnp.sum(weight * gap, axis=0),
        )

    def sweep(tile, feats, wq, fresh):
        qa, qb = 2 * wq, 2 * wq + 1
        query_a, query_b = feats[at_block(qa), :], feats[at_block(qb), :]

        def full(i, c):
            state_a, state_b = c
            for kb in (2 * i, 2 * i + 1):
                state_a = tile(kb, qa, query_a, state_a, False)
                state_b = tile(kb, qb, query_b, state_b, False)
            return state_a, state_b

        state_a, state_b = fresh, fresh
        for i in range(wq):
            state_a, state_b = full(i, (state_a, state_b))
        state_a = tile(qa, qa, query_a, state_a, True)
        state_b = tile(qa, qb, query_b, state_b, False)
        state_b = tile(qb, qb, query_b, state_b, True)
        return (qa, state_a), (qb, state_b)

    def loop(n, f, init):
        for i in range(n):
            init = f(i, init)
        return init

    low = jnp.full((8, BLK), NEG, F32)
    zero = jnp.zeros((8, BLK), F32)

    @pl.when(active)
    def _():
        await_bytes(s_all, s_recv)

        def turn(b, c):
            s_turn[:, at_block(b)] = s_all[at_block(b), :].T
            col[at_block(b), :] = jnp.zeros((BLK, HD), F32)
            return c

        lax.fori_loop(0, 2 * wide, turn, 0)

        def student_block(wq, c):
            for q, (top, total) in sweep(student_tile, s_all, wq, (low, zero)):
                peak = jnp.max(top, axis=0, keepdims=True)
                total = jnp.sum(total * jnp.exp2(top - peak), axis=0, keepdims=True)
                lse_s[q] = jnp.broadcast_to(peak + jnp.log2(total), (8, BLK))
            return c

        loop(wide, student_block, 0)

        await_bytes(t_all, t_recv)

        def teacher_block(wq, loss_row):
            for q, (top, total, cross) in sweep(teacher_tile, t_all, wq, (low, zero, zero)):
                peak = jnp.max(top, axis=0, keepdims=True)
                again = jnp.exp2(top - peak)
                total = jnp.sum(total * again, axis=0, keepdims=True)
                cross = jnp.sum(cross * again, axis=0, keepdims=True)
                lse = jnp.broadcast_to(peak + jnp.log2(total), (8, BLK))
                lse_t[q] = lse
                loss_row = loss_row + (cross / total - lse + lse_s[q])
            return loss_row

        loss_row = loop(wide, teacher_block, zero)
        mine = jnp.full((8, HD), jnp.sum(loss_row) * 0.125, F32)
        l_mine[...] = mine
        l_seq[me_s] = mine

        def loss_out(i, c):
            s = lax.rem(me_s + 1 + i, ns)
            send(l_mine, l_seq.at[me_s], l_send.at[0], l_recv.at[0], s, me_g)
            return c

        lax.fori_loop(0, ns - 1, loss_out, 0)

        def diff(kb, q):
            t = tile_of(kb, q)
            ours = w_s[t].reshape(deep) * jnp.exp2(top_s[t] - lse_s[q])
            theirs = w_t[t].reshape(deep) * jnp.exp2(top_t[t] - lse_t[q])
            return (ours - theirs).reshape(BLK, BLK).astype(BF16)

        def add(kb, q, query, row):
            d = diff(kb, q)
            col[at_block(kb), :] += jnp.dot(d, query, preferred_element_type=F32)
            return row + jnp.dot(s_turn[:, at_block(kb)], d, preferred_element_type=F32)

        def grad_block(step, c):
            wq = wide - 1 - step
            qa, qb = 2 * wq, 2 * wq + 1
            query_a, query_b = s_all[at_block(qa), :], s_all[at_block(qb), :]

            def full(i, c):
                row_a, row_b = c
                for kb in (2 * i, 2 * i + 1):
                    row_a = add(kb, qa, query_a, row_a)
                    row_b = add(kb, qb, query_b, row_b)
                return row_a, row_b

            none = jnp.zeros((HD, BLK), F32)
            row_a, row_b = none, none
            for i in range(wq):
                row_a, row_b = full(i, (row_a, row_b))
            row_a = add(qa, qa, query_a, row_a)
            row_b = add(qa, qb, query_b, row_b)
            row_b = add(qb, qb, query_b, row_b)
            for q, row in ((qa, row_a), (qb, row_b)):
                block = (col[at_block(q), :] + row.T) * (1.0 / math.sqrt(HD))
                back[at_block(q), :] = block.astype(BF16)
            for j in range(per_blk):
                s = wq * per_blk + j
                src = back.at[pl.ds(pl.multiple_of(s * rows, rows), rows), :]
                dst = grads.at[my_p, :, pl.ds(pl.multiple_of(my_rl * HD, HD), HD)]

                @pl.when(s != me_s)
                def _():
                    send(src, dst, g_send, g_recv, s, me_g)

                @pl.when(s == me_s)
                def _():
                    pltpu.make_async_copy(src, dst, g_recv).start()

            return c

        loop(wide, grad_block, 0)
        await_bytes(l_seq.at[pl.ds(0, 3 * rels - 1)], l_recv.at[0])

    @pl.when(jnp.logical_not(active))
    def _():
        await_bytes(l_seq.at[pl.ds(0, 3 * rels)], l_recv.at[0])

    group = jnp.zeros((8, HD), F32)
    for s in range(ns):
        if owner_of_static(s)[0] < 3:
            group = group + l_seq[s]
    l_head[me_g] = group
    for step in range(1, nh):
        send(l_head.at[me_g], l_head.at[me_g], l_send.at[1], l_recv.at[1], me_s, lax.rem(me_g + step, nh))
    await_bytes(grads, g_recv)
    await_bytes(l_head.at[pl.ds(0, nh - 1)], l_recv.at[1])
    total = l_head[0]
    for g in range(1, nh):
        total = total + l_head[g]
    loss[0] = total[0, 0] * (1.0 / (LOG2E * 3.0 * rel_all * tokens))

    await_bytes(teacher.at[:, pl.ds(0, rows - sub), :], p1_send)

    @pl.when(active)
    def _():
        await_bytes(back.at[pl.ds(0, (3 * rels - 1) * rows), :], s_send)
        await_bytes(back.at[pl.ds(0, (ns - 1) * rows), :], g_send)
        await_bytes(t_all.at[pl.ds(0, (3 * rel_all - 1) * sub), :], p2_send)
        await_bytes(l_seq.at[pl.ds(0, ns - 1)], l_send.at[0])

    @pl.when(jnp.logical_not(active))
    def _():
        await_bytes(back.at[pl.ds(0, 3 * rels * rows), :], s_send)
        await_bytes(t_all.at[pl.ds(0, 3 * rel_all * sub), :], p2_send)

    await_bytes(l_head.at[pl.ds(0, nh - 1)], l_send.at[1])


def solution(mesh):
    ns = mesh.shape["seq"]
    nh = mesh.shape["head"]

    def body(teacher, student, table):
        rows, _, width = teacher.shape
        swidth = student.shape[2]
        sub = rows // nh
        rel_all = swidth // HD * nh
        tokens = rows * ns
        blocks = tokens // BLK
        tiles = blocks * (blocks + 1) // 2
        dma = pltpu.SemaphoreType.DMA
        loss, grads = pl.pallas_call(
            functools.partial(kernel, ns, nh),
            out_shape=(
                jax.ShapeDtypeStruct((1,), F32),
                jax.ShapeDtypeStruct((3, rows, swidth), BF16),
            ),
            in_specs=[
                pl.BlockSpec(memory_space=pltpu.HBM),
                pl.BlockSpec(memory_space=pltpu.HBM),
                pl.BlockSpec(memory_space=pltpu.HBM),
            ],
            out_specs=(
                pl.BlockSpec(memory_space=pltpu.SMEM),
                pl.BlockSpec(memory_space=pltpu.HBM),
            ),
            scratch_shapes=[pltpu.SMEM(table.shape, jnp.int32)]
            + [pltpu.VMEM((nh, sub, width), BF16)] * 3
            + [pltpu.VMEM((width // HD * nh, sub, HD), BF16)] * 3
            + [pltpu.VMEM((rel_all, sub, GRP * HD), BF16)] * 3
            + [
                pltpu.VMEM((tokens, GRP * HD), BF16),
                pltpu.VMEM((tokens, HD), BF16),
                pltpu.VMEM((HD, tokens), BF16),
                pltpu.VMEM((tiles, BLK, BLK), F32),
                pltpu.VMEM((tiles, BLK, BLK), F32),
                pltpu.VMEM((tiles, BLK, BLK), F32),
                pltpu.VMEM((tiles, 8, BLK), F32),
                pltpu.VMEM((tiles, 8, BLK), F32),
                pltpu.VMEM((blocks, 8, BLK), F32),
                pltpu.VMEM((blocks, 8, BLK), F32),
                pltpu.VMEM((tokens, HD), F32),
                pltpu.VMEM((tokens, HD), BF16),
                pltpu.VMEM((8, HD), F32),
                pltpu.VMEM((ns, 8, HD), F32),
                pltpu.VMEM((nh, 8, HD), F32),
                dma, dma, dma((3,)), dma, dma, dma, dma, dma, dma, dma((2,)), dma((2,)),
                pltpu.SemaphoreType.REGULAR,
            ],
            compiler_params=pltpu.CompilerParams(
                has_side_effects=True, collective_id=0, vmem_limit_bytes=60 * 1024 * 1024
            ),
            cost_estimate=pl.CostEstimate(
                flops=tokens * tokens * 1280, bytes_accessed=4 * 1024 * 1024,
                transcendentals=tokens * tokens,
            ),
            name="relations",
        )(table, jnp.transpose(teacher, (1, 0, 2)), jnp.transpose(student, (1, 0, 2)))
        return loss.reshape(()), jnp.transpose(grads, (1, 0, 2))

    return jax.shard_map(
        body,
        mesh=mesh,
        in_specs=(P("seq", None, "head"), P("seq", None, "head"), P()),
        out_specs=(P(), P("seq", None, "head")),
        check_vma=False,
    )
```

```python
import functools
import math

import jax
import jax.numpy as jnp
from jax import lax
from jax.experimental import pallas as pl
from jax.experimental.pallas import tpu as pltpu
from jax.sharding import PartitionSpec as P

HD = 128
GRP = 2
BLK = 256
CH = 256
NEG = -1e30
MESH = pl.DeviceIdType.MESH
F32 = jnp.float32
BF16 = jnp.bfloat16
LOG2E = math.log2(math.e)


def owner_seq(p, rl):
    return 4 * rl + lax.rem(p + rl + 1, 4)


def owner_of_static(s):
    rl = s // 4
    p = (s % 4 - rl - 1) % 4
    return p, rl


def await_bytes(ref, sem):
    pltpu.make_async_copy(ref, ref, sem).wait()


def dot_t(a, b):
    return lax.dot_general(a, b, (((1,), (1,)), ((), ())), preferred_element_type=F32)


def kernel(
    ns, nh, table_hbm, teacher, student, loss, grads, table,
    got0, got1, got2, flat0, flat1, flat2, stage0, stage1, stage2,
    t_all, s_all, s_turn, log_s, w_s, w_t, top_s, top_t, lse_s, lse_t, rows_turned, back,
    l_mine, l_seq, l_head,
    tab_sem, p1_send, p1_recv, s_send, s_recv, p2_send, t_recv, g_send, g_recv, l_send, l_recv, all_in,
):
    rows = teacher.shape[1]
    width = teacher.shape[2]
    slots = width // HD
    sub = rows // nh
    rels = student.shape[2] // HD
    rel_all = rels * nh
    tokens = rows * ns
    wide = tokens // (2 * BLK)
    per_blk = 2 * BLK // rows
    me_s = lax.axis_index("seq")
    me_g = lax.axis_index("head")
    my_rl = me_s // 4
    my_p = lax.rem(lax.rem(me_s, 4) - my_rl + 7, 4)
    active = my_p < 3
    got = (got0, got1, got2)
    flat = (flat0, flat1, flat2)
    stage = (stage0, stage1, stage2)

    def send(src, dst, ssem, rsem, s, g):
        pltpu.make_async_remote_copy(
            src_ref=src, dst_ref=dst, send_sem=ssem, recv_sem=rsem,
            device_id=(s, g), device_id_type=MESH,
        ).start()

    barrier = pltpu.get_barrier_semaphore()

    def greet(sem, along_seq):
        def one(i, c):
            if along_seq:
                to = (lax.rem(me_s + i, ns), me_g)
            else:
                to = (me_s, lax.rem(me_g + i, nh))
            pl.semaphore_signal(sem, inc=1, device_id=to, device_id_type=MESH)
            return c

        lax.fori_loop(1, ns if along_seq else nh, one, 0)

    greet(barrier, False)
    greet(barrier, True)
    table_copy = pltpu.make_async_copy(table_hbm, table, tab_sem)
    table_copy.start()
    pl.semaphore_wait(barrier, ns + nh - 2)

    for p in range(3):
        for step in range(1, nh):
            g = lax.rem(me_g + step, nh)
            send(
                teacher.at[p, pl.ds(g * sub, sub), :], got[p].at[me_g],
                p1_send, p1_recv.at[p], me_s, g,
            )
        pltpu.make_async_copy(
            teacher.at[p, pl.ds(me_g * sub, sub), :], got[p].at[me_g], p1_recv.at[p]
        ).start()

    greet(all_in, False)

    def student_out(i, c):
        q = lax.rem(i + me_s, 3 * rels)
        p = q // rels
        rl = lax.rem(q, rels)
        s = owner_seq(p, rl)
        src = student.at[p, :, pl.ds(pl.multiple_of(rl * HD, HD), HD)]
        dst = s_all.at[pl.ds(pl.multiple_of(me_s * rows, rows), rows), :]

        @pl.when(s != me_s)
        def _():
            send(src, dst, s_send, s_recv, s, me_g)

        @pl.when(s == me_s)
        def _():
            pltpu.make_async_copy(src, dst, s_recv).start()

        return c

    lax.fori_loop(0, 3 * rels, student_out, 0)
    table_copy.wait()
    pl.semaphore_wait(all_in, nh - 1)

    for p in range(3):
        await_bytes(got[p], p1_recv.at[p])
        for h in range(slots * nh):
            lane = h % slots * HD
            flat[p][h] = got[p][h // slots, :, lane : lane + HD]

        def relation_out(i, c):
            r = lax.rem(i + 2 * me_s + rels * me_g, rel_all)
            for k in range(GRP):
                stage[p][r, :, k * HD : (k + 1) * HD] = flat[p][table[GRP * r + k]]
            g = r // rels
            s = owner_seq(p, lax.rem(r, rels))
            src = stage[p].at[r]
            dst = t_all.at[pl.ds(pl.multiple_of(me_s * rows + me_g * sub, sub), sub), :]
            here = jnp.logical_and(s == me_s, g == me_g)

            @pl.when(jnp.logical_not(here))
            def _():
                send(src, dst, p2_send, t_recv.at[me_s // per_blk], s, g)

            @pl.when(here)
            def _():
                pltpu.make_async_copy(src, dst, t_recv.at[me_s // per_blk]).start()

            return c

        lax.fori_loop(0, rel_all, relation_out, 0)

    scale_t = LOG2E / math.sqrt(GRP * HD)
    scale_s = LOG2E / math.sqrt(HD)
    key_row = lax.broadcasted_iota(jnp.int32, (BLK, BLK), 0)
    query_col = lax.broadcasted_iota(jnp.int32, (BLK, BLK), 1)
    deep = (CH // 8, 8, BLK)

    def at_block(b):
        return pl.ds(pl.multiple_of(b * BLK, BLK), BLK)

    def tile_of(kb, qb):
        return qb * (qb + 1) // 2 + kb

    def logits(feats, kb, query, scale, diagonal):
        out = dot_t(feats[at_block(kb), :], query) * scale
        if diagonal:
            out = jnp.where(key_row <= query_col, out, NEG)
        return [out[c * CH : (c + 1) * CH].reshape(deep) for c in range(BLK // CH)]

    def student_tile(kb, qb, query, state, diagonal):
        top, total = state
        t = tile_of(kb, qb)
        for c, logit in enumerate(logits(s_all, kb, query, scale_s, diagonal)):
            new = jnp.maximum(top, jnp.max(logit, axis=0))
            weight = jnp.exp2(logit - new)
            log_s[t, c * CH : (c + 1) * CH, :] = logit.reshape(CH, BLK)
            w_s[t, c * CH : (c + 1) * CH, :] = weight.reshape(CH, BLK)
            top_s[t, c] = new
            total = total * jnp.exp2(top - new) + jnp.sum(weight, axis=0)
            top = new
        return top, total

    def teacher_tile(kb, qb, query, state, diagonal):
        top, total, cross = state
        t = tile_of(kb, qb)
        for c, logit in enumerate(logits(t_all, kb, query, scale_t, diagonal)):
            new = jnp.maximum(top, jnp.max(logit, axis=0))
            weight = jnp.exp2(logit - new)
            w_t[t, c * CH : (c + 1) * CH, :] = weight.reshape(CH, BLK)
            top_t[t, c] = new
            again = jnp.exp2(top - new)
            gap = logit - log_s[t, c * CH : (c + 1) * CH, :].reshape(deep)
            total = total * again + jnp.sum(weight, axis=0)
            cross = cross * again + jnp.sum(weight * gap, axis=0)
            top = new
        return top, total, cross

    def sweep(tile, feats, wq, fresh):
        qa, qb = 2 * wq, 2 * wq + 1
        query_a, query_b = feats[at_block(qa), :], feats[at_block(qb), :]

        def full(i, c):
            state_a, state_b = c
            for kb in (2 * i, 2 * i + 1):
                state_a = tile(kb, qa, query_a, state_a, False)
                state_b = tile(kb, qb, query_b, state_b, False)
            return state_a, state_b

        state_a, state_b = fresh, fresh
        for i in range(wq):
            state_a, state_b = full(i, (state_a, state_b))
        state_a = tile(qa, qa, query_a, state_a, True)
        state_b = tile(qa, qb, query_b, state_b, False)
        state_b = tile(qb, qb, query_b, state_b, True)
        return (qa, state_a), (qb, state_b)

    def loop(n, f, init):
        for i in range(n):
            init = f(i, init)
        return init

    low = jnp.full((8, BLK), NEG, F32)
    zero = jnp.zeros((8, BLK), F32)

    @pl.when(active)
    def _():
        await_bytes(s_all, s_recv)

        def turn(b, c):
            s_turn[:, at_block(b)] = s_all[at_block(b), :].T
            return c

        lax.fori_loop(0, 2 * wide, turn, 0)

        def student_block(wq, c):
            for q, (top, total) in sweep(student_tile, s_all, wq, (low, zero)):
                peak = jnp.max(top, axis=0, keepdims=True)
                total = jnp.sum(total * jnp.exp2(top - peak), axis=0, keepdims=True)
                lse_s[q] = jnp.broadcast_to(peak + jnp.log2(total), (8, BLK))
            return c

        loop(wide, student_block, 0)

        def teacher_block(wq, loss_row):
            await_bytes(t_all.at[pl.ds(2 * wq * BLK, 2 * BLK), :], t_recv.at[wq])
            for q, (top, total, cross) in sweep(teacher_tile, t_all, wq, (low, zero, zero)):
                peak = jnp.max(top, axis=0, keepdims=True)
                again = jnp.exp2(top - peak)
                total = jnp.sum(total * again, axis=0, keepdims=True)
                cross = jnp.sum(cross * again, axis=0, keepdims=True)
                lse = jnp.broadcast_to(peak + jnp.log2(total), (8, BLK))
                lse_t[q] = lse
                loss_row = loss_row + (cross / total - lse + lse_s[q])
            return loss_row

        loss_row = loop(wide, teacher_block, zero)
        mine = jnp.full((8, HD), jnp.sum(loss_row) * 0.125, F32)
        l_mine[...] = mine
        l_seq[me_s] = mine

        def loss_out(i, c):
            s = lax.rem(me_s + 1 + i, ns)
            send(l_mine, l_seq.at[me_s], l_send.at[0], l_recv.at[0], s, me_g)
            return c

        lax.fori_loop(0, ns - 1, loss_out, 0)

        def diff(kb, q):
            t = tile_of(kb, q)
            parts = []
            for c in range(BLK // CH):
                ours = w_s[t, c * CH : (c + 1) * CH, :].reshape(deep) * jnp.exp2(top_s[t, c] - lse_s[q])
                theirs = w_t[t, c * CH : (c + 1) * CH, :].reshape(deep) * jnp.exp2(top_t[t, c] - lse_t[q])
                parts.append((ours - theirs).reshape(CH, BLK).astype(BF16))
            return jnp.concatenate(parts, axis=0)

        for kb in range(2 * wide):
            keys_turned = s_turn[:, at_block(kb)]
            col = jnp.zeros((BLK, HD), F32)
            for q in range(kb, 2 * wide):
                d = diff(kb, q)
                col = col + jnp.dot(d, s_all[at_block(q), :], preferred_element_type=F32)
                row = jnp.dot(keys_turned, d, preferred_element_type=F32)
                if kb > 0:
                    row = row + rows_turned[:, at_block(q)]
                if q > kb:
                    rows_turned[:, at_block(q)] = row
                else:
                    last = row
            back[at_block(kb), :] = ((col + last.T) * (1.0 / math.sqrt(HD))).astype(BF16)
            for j in range(BLK // rows):
                s = kb * (BLK // rows) + j
                src = back.at[pl.ds(s * rows, rows), :]
                dst = grads.at[my_p, :, pl.ds(pl.multiple_of(my_rl * HD, HD), HD)]

                @pl.when(s != me_s)
                def _():
                    send(src, dst, g_send, g_recv, s, me_g)

                @pl.when(s == me_s)
                def _():
                    pltpu.make_async_copy(src, dst, g_recv).start()

        await_bytes(l_seq.at[pl.ds(0, 3 * rels - 1)], l_recv.at[0])

    @pl.when(jnp.logical_not(active))
    def _():
        await_bytes(l_seq.at[pl.ds(0, 3 * rels)], l_recv.at[0])

    group = jnp.zeros((8, HD), F32)
    for s in range(ns):
        if owner_of_static(s)[0] < 3:
            group = group + l_seq[s]
    l_head[me_g] = group
    for step in range(1, nh):
        send(l_head.at[me_g], l_head.at[me_g], l_send.at[1], l_recv.at[1], me_s, lax.rem(me_g + step, nh))
    await_bytes(grads, g_recv)
    await_bytes(l_head.at[pl.ds(0, nh - 1)], l_recv.at[1])
    total = l_head[0]
    for g in range(1, nh):
        total = total + l_head[g]
    loss[0] = total[0, 0] * (1.0 / (LOG2E * 3.0 * rel_all * tokens))

    await_bytes(teacher.at[:, pl.ds(0, rows - sub), :], p1_send)

    @pl.when(active)
    def _():
        await_bytes(back.at[pl.ds(0, (3 * rels - 1) * rows), :], s_send)
        await_bytes(back.at[pl.ds(0, (ns - 1) * rows), :], g_send)
        await_bytes(t_all.at[pl.ds(0, (3 * rel_all - 1) * sub), :], p2_send)
        await_bytes(l_seq.at[pl.ds(0, ns - 1)], l_send.at[0])

    @pl.when(jnp.logical_not(active))
    def _():
        await_bytes(back.at[pl.ds(0, 3 * rels * rows), :], s_send)
        await_bytes(t_all.at[pl.ds(0, 3 * rel_all * sub), :], p2_send)

    await_bytes(l_head.at[pl.ds(0, nh - 1)], l_send.at[1])


def solution(mesh):
    ns = mesh.shape["seq"]
    nh = mesh.shape["head"]

    def body(teacher, student, table):
        rows, _, width = teacher.shape
        swidth = student.shape[2]
        sub = rows // nh
        rel_all = swidth // HD * nh
        tokens = rows * ns
        blocks = tokens // BLK
        tiles = blocks * (blocks + 1) // 2
        dma = pltpu.SemaphoreType.DMA
        loss, grads = pl.pallas_call(
            functools.partial(kernel, ns, nh),
            out_shape=(
                jax.ShapeDtypeStruct((1,), F32),
                jax.ShapeDtypeStruct((3, rows, swidth), BF16),
            ),
            in_specs=[
                pl.BlockSpec(memory_space=pltpu.HBM),
                pl.BlockSpec(memory_space=pltpu.HBM),
                pl.BlockSpec(memory_space=pltpu.HBM),
            ],
            out_specs=(
                pl.BlockSpec(memory_space=pltpu.SMEM),
                pl.BlockSpec(memory_space=pl.ANY),
            ),
            scratch_shapes=[pltpu.SMEM(table.shape, jnp.int32)]
            + [pltpu.VMEM((nh, sub, width), BF16)] * 3
            + [pltpu.VMEM((width // HD * nh, sub, HD), BF16)] * 3
            + [pltpu.VMEM((rel_all, sub, GRP * HD), BF16)] * 3
            + [
                pltpu.VMEM((tokens, GRP * HD), BF16),
                pltpu.VMEM((tokens, HD), BF16),
                pltpu.VMEM((HD, tokens), BF16),
                pltpu.VMEM((tiles, BLK, BLK), F32),
                pltpu.VMEM((tiles, BLK, BLK), F32),
                pltpu.VMEM((tiles, BLK, BLK), F32),
                pltpu.VMEM((tiles, BLK // CH, 8, BLK), F32),
                pltpu.VMEM((tiles, BLK // CH, 8, BLK), F32),
                pltpu.VMEM((blocks, 8, BLK), F32),
                pltpu.VMEM((blocks, 8, BLK), F32),
                pltpu.VMEM((HD, tokens), F32),
                pltpu.VMEM((tokens, HD), BF16),
                pltpu.VMEM((8, HD), F32),
                pltpu.VMEM((ns, 8, HD), F32),
                pltpu.VMEM((nh, 8, HD), F32),
                dma, dma, dma((3,)), dma, dma, dma, dma((blocks // 2,)), dma, dma, dma((2,)), dma((2,)),
                pltpu.SemaphoreType.REGULAR,
            ],
            compiler_params=pltpu.CompilerParams(
                has_side_effects=True, collective_id=0, vmem_limit_bytes=48 * 1024 * 1024
            ),
            cost_estimate=pl.CostEstimate(
                flops=tokens * tokens * 1280, bytes_accessed=4 * 1024 * 1024,
                transcendentals=tokens * tokens,
            ),
            name="relations",
        )(*[pltpu.with_memory_space_constraint(x, pltpu.HBM) for x in (table, jnp.transpose(teacher, (1, 0, 2)), jnp.transpose(student, (1, 0, 2)))])
        return loss.reshape(()), jnp.transpose(grads, (1, 0, 2))

    return jax.shard_map(
        body,
        mesh=mesh,
        in_specs=(P("seq", None, "head"), P("seq", None, "head"), P()),
        out_specs=(P(), P("seq", None, "head")),
        check_vma=False,
    )
```

```python
import functools
import math

import jax
import jax.numpy as jnp
from jax import lax
from jax.experimental import pallas as pl
from jax.experimental.pallas import tpu as pltpu
from jax.sharding import PartitionSpec as P

HD = 128
GRP = 2
BLK = 256
CH = 256
NEG = -1e30
MESH = pl.DeviceIdType.MESH
FAR_FIRST = [(2, 1), (1, 1), (3, 1), (2, 0), (0, 1), (1, 0), (3, 0)]
F32 = jnp.float32
BF16 = jnp.bfloat16
LOG2E = math.log2(math.e)


def owner_seq(p, rl):
    return 4 * rl + lax.rem(p + rl + 1, 4)


def owner_of_static(s):
    rl = s // 4
    p = (s % 4 - rl - 1) % 4
    return p, rl


def await_bytes(ref, sem):
    pltpu.make_async_copy(ref, ref, sem).wait()


def dot_t(a, b):
    return lax.dot_general(a, b, (((1,), (1,)), ((), ())), preferred_element_type=F32)


def kernel(
    ns, nh, table_hbm, teacher, student, loss, grads, table,
    got0, got1, got2, flat0, flat1, flat2, stage0, stage1, stage2,
    t_all, s_all, s_turn, log_s, w_s, w_t, top_s, top_t, lse_s, lse_t, rows_turned, back,
    l_mine, l_seq, l_head,
    tab_sem, p1_send, p1_recv, s_send, s_recv, p2_send, t_recv, g_send, g_recv, l_send, l_recv, all_in, t_near, s_near, pre_sem,
):
    rows = teacher.shape[1]
    width = teacher.shape[2]
    slots = width // HD
    sub = rows // nh
    rels = student.shape[2] // HD
    rel_all = rels * nh
    tokens = rows * ns
    wide = tokens // (2 * BLK)
    per_blk = 2 * BLK // rows
    me_s = lax.axis_index("seq")
    me_g = lax.axis_index("head")
    my_rl = me_s // 4
    my_p = lax.rem(lax.rem(me_s, 4) - my_rl + 7, 4)
    active = my_p < 3
    got = (got0, got1, got2)
    flat = (flat0, flat1, flat2)
    stage = (stage0, stage1, stage2)

    def send(src, dst, ssem, rsem, s, g):
        pltpu.make_async_remote_copy(
            src_ref=src, dst_ref=dst, send_sem=ssem, recv_sem=rsem,
            device_id=(s, g), device_id_type=MESH,
        ).start()

    barrier = pltpu.get_barrier_semaphore()

    def greet(sem, along_seq):
        def one(i, c):
            if along_seq:
                to = (lax.rem(me_s + i, ns), me_g)
            else:
                to = (me_s, lax.rem(me_g + i, nh))
            pl.semaphore_signal(sem, inc=1, device_id=to, device_id_type=MESH)
            return c

        lax.fori_loop(1, ns if along_seq else nh, one, 0)

    greet(barrier, False)
    greet(barrier, True)
    table_copy = pltpu.make_async_copy(table_hbm, table, tab_sem)
    table_copy.start()
    pre_t = pltpu.make_async_copy(teacher, t_near, pre_sem.at[0])
    pre_s = pltpu.make_async_copy(student, s_near, pre_sem.at[1])
    pre_t.start()
    pre_s.start()
    pl.semaphore_wait(barrier, ns + nh - 2)
    pre_t.wait()
    pre_s.wait()
    teacher, student = t_near, s_near

    for p in range(3):
        for step in range(1, nh):
            dy, dx = FAR_FIRST[step - 1] if nh == 8 else (step // 2, step % 2)
            g = lax.rem(me_g // 2 + dy, nh // 2) * 2 + lax.rem(me_g + dx, 2)
            send(
                teacher.at[p, pl.ds(g * sub, sub), :], got[p].at[me_g],
                p1_send, p1_recv.at[p], me_s, g,
            )
        pltpu.make_async_copy(
            teacher.at[p, pl.ds(me_g * sub, sub), :], got[p].at[me_g], p1_recv.at[p]
        ).start()

    greet(all_in, False)

    def student_out(i, c):
        q = lax.rem(i + me_s, 3 * rels)
        p = q // rels
        rl = lax.rem(q, rels)
        s = owner_seq(p, rl)
        src = student.at[p, :, pl.ds(pl.multiple_of(rl * HD, HD), HD)]
        dst = s_all.at[pl.ds(pl.multiple_of(me_s * rows, rows), rows), :]

        @pl.when(s != me_s)
        def _():
            send(src, dst, s_send, s_recv, s, me_g)

        @pl.when(s == me_s)
        def _():
            pltpu.make_async_copy(src, dst, s_recv).start()

        return c

    lax.fori_loop(0, 3 * rels, student_out, 0)
    table_copy.wait()
    pl.semaphore_wait(all_in, nh - 1)

    for p in range(3):
        await_bytes(got[p], p1_recv.at[p])
        for h in range(slots * nh):
            lane = h % slots * HD
            flat[p][h] = got[p][h // slots, :, lane : lane + HD]

        def relation_out(i, c):
            r = lax.rem(i + 2 * me_s + rels * me_g, rel_all)
            for k in range(GRP):
                stage[p][r, :, k * HD : (k + 1) * HD] = flat[p][table[GRP * r + k]]
            g = r // rels
            s = owner_seq(p, lax.rem(r, rels))
            src = stage[p].at[r]
            dst = t_all.at[pl.ds(pl.multiple_of(me_s * rows + me_g * sub, sub), sub), :]
            here = jnp.logical_and(s == me_s, g == me_g)

            @pl.when(jnp.logical_not(here))
            def _():
                send(src, dst, p2_send, t_recv.at[me_s // per_blk], s, g)

            @pl.when(here)
            def _():
                pltpu.make_async_copy(src, dst, t_recv.at[me_s // per_blk]).start()

            return c

        lax.fori_loop(0, rel_all, relation_out, 0)

    scale_t = LOG2E / math.sqrt(GRP * HD)
    scale_s = LOG2E / math.sqrt(HD)
    key_row = lax.broadcasted_iota(jnp.int32, (BLK, BLK), 0)
    query_col = lax.broadcasted_iota(jnp.int32, (BLK, BLK), 1)
    deep = (CH // 8, 8, BLK)

    def at_block(b):
        return pl.ds(pl.multiple_of(b * BLK, BLK), BLK)

    def tile_of(kb, qb):
        return qb * (qb + 1) // 2 + kb

    def logits(feats, kb, query, scale, diagonal):
        out = dot_t(feats[at_block(kb), :], query) * scale
        if diagonal:
            out = jnp.where(key_row <= query_col, out, NEG)
        return [out[c * CH : (c + 1) * CH].reshape(deep) for c in range(BLK // CH)]

    def student_tile(kb, qb, query, state, diagonal):
        top, total = state
        t = tile_of(kb, qb)
        for c, logit in enumerate(logits(s_all, kb, query, scale_s, diagonal)):
            new = jnp.maximum(top, jnp.max(logit, axis=0))
            weight = jnp.exp2(logit - new)
            log_s[t, c * CH : (c + 1) * CH, :] = logit.reshape(CH, BLK)
            w_s[t, c * CH : (c + 1) * CH, :] = weight.reshape(CH, BLK)
            top_s[t, c] = new
            total = total * jnp.exp2(top - new) + jnp.sum(weight, axis=0)
            top = new
        return top, total

    def teacher_tile(kb, qb, query, state, diagonal):
        top, total, cross = state
        t = tile_of(kb, qb)
        for c, logit in enumerate(logits(t_all, kb, query, scale_t, diagonal)):
            new = jnp.maximum(top, jnp.max(logit, axis=0))
            weight = jnp.exp2(logit - new)
            w_t[t, c * CH : (c + 1) * CH, :] = weight.reshape(CH, BLK)
            top_t[t, c] = new
            again = jnp.exp2(top - new)
            gap = logit - log_s[t, c * CH : (c + 1) * CH, :].reshape(deep)
            total = total * again + jnp.sum(weight, axis=0)
            cross = cross * again + jnp.sum(weight * gap, axis=0)
            top = new
        return top, total, cross

    def sweep(tile, feats, wq, fresh):
        qa, qb = 2 * wq, 2 * wq + 1
        query_a, query_b = feats[at_block(qa), :], feats[at_block(qb), :]

        def full(i, c):
            state_a, state_b = c
            for kb in (2 * i, 2 * i + 1):
                state_a = tile(kb, qa, query_a, state_a, False)
                state_b = tile(kb, qb, query_b, state_b, False)
            return state_a, state_b

        state_a, state_b = fresh, fresh
        for i in range(wq):
            state_a, state_b = full(i, (state_a, state_b))
        state_a = tile(qa, qa, query_a, state_a, True)
        state_b = tile(qa, qb, query_b, state_b, False)
        state_b = tile(qb, qb, query_b, state_b, True)
        return (qa, state_a), (qb, state_b)

    def loop(n, f, init):
        for i in range(n):
            init = f(i, init)
        return init

    low = jnp.full((8, BLK), NEG, F32)
    zero = jnp.zeros((8, BLK), F32)

    @pl.when(active)
    def _():
        await_bytes(s_all, s_recv)

        def turn(b, c):
            s_turn[:, at_block(b)] = s_all[at_block(b), :].T
            return c

        lax.fori_loop(0, 2 * wide, turn, 0)

        def student_block(wq, c):
            for q, (top, total) in sweep(student_tile, s_all, wq, (low, zero)):
                peak = jnp.max(top, axis=0, keepdims=True)
                total = jnp.sum(total * jnp.exp2(top - peak), axis=0, keepdims=True)
                lse_s[q] = jnp.broadcast_to(peak + jnp.log2(total), (8, BLK))
            return c

        loop(wide, student_block, 0)

        def teacher_block(wq, loss_row):
            await_bytes(t_all.at[pl.ds(2 * wq * BLK, 2 * BLK), :], t_recv.at[wq])
            for q, (top, total, cross) in sweep(teacher_tile, t_all, wq, (low, zero, zero)):
                peak = jnp.max(top, axis=0, keepdims=True)
                again = jnp.exp2(top - peak)
                total = jnp.sum(total * again, axis=0, keepdims=True)
                cross = jnp.sum(cross * again, axis=0, keepdims=True)
                lse = jnp.broadcast_to(peak + jnp.log2(total), (8, BLK))
                lse_t[q] = lse
                loss_row = loss_row + (cross / total - lse + lse_s[q])
            return loss_row

        loss_row = loop(wide, teacher_block, zero)
        mine = loss_row[:, :HD] + loss_row[:, HD:]
        l_mine[...] = mine
        l_seq[me_s] = mine

        def loss_out(i, c):
            s = 4 * (i // 4) + lax.rem(me_s + i, 4)

            @pl.when(s != me_s)
            def _():
                send(l_mine, l_seq.at[me_s], l_send.at[0], l_recv.at[0], s, me_g)

            return c

        lax.fori_loop(0, ns, loss_out, 0)

        def diff(kb, q):
            t = tile_of(kb, q)
            parts = []
            for c in range(BLK // CH):
                ours = w_s[t, c * CH : (c + 1) * CH, :].reshape(deep) * jnp.exp2(top_s[t, c] - lse_s[q])
                theirs = w_t[t, c * CH : (c + 1) * CH, :].reshape(deep) * jnp.exp2(top_t[t, c] - lse_t[q])
                parts.append((ours - theirs).reshape(CH, BLK).astype(BF16))
            return jnp.concatenate(parts, axis=0)

        for kb in range(2 * wide):
            keys_turned = s_turn[:, at_block(kb)]
            col = jnp.zeros((BLK, HD), F32)
            for q in range(kb, 2 * wide):
                d = diff(kb, q)
                col = col + jnp.dot(d, s_all[at_block(q), :], preferred_element_type=F32)
                row = jnp.dot(keys_turned, d, preferred_element_type=F32)
                if kb > 0:
                    row = row + rows_turned[:, at_block(q)]
                if q > kb:
                    rows_turned[:, at_block(q)] = row
                else:
                    last = row
            back[at_block(kb), :] = ((col + last.T) * (1.0 / math.sqrt(HD))).astype(BF16)
            for j in range(BLK // rows):
                s = kb * (BLK // rows) + j
                src = back.at[pl.ds(s * rows, rows), :]
                dst = grads.at[my_p, :, pl.ds(pl.multiple_of(my_rl * HD, HD), HD)]

                @pl.when(s != me_s)
                def _():
                    send(src, dst, g_send, g_recv, s, me_g)

                @pl.when(s == me_s)
                def _():
                    pltpu.make_async_copy(src, dst, g_recv).start()

        await_bytes(l_seq.at[pl.ds(0, 3 * rels - 1)], l_recv.at[0])

    @pl.when(jnp.logical_not(active))
    def _():
        await_bytes(l_seq.at[pl.ds(0, 3 * rels)], l_recv.at[0])

    group = jnp.zeros((8, HD), F32)
    for s in range(ns):
        if owner_of_static(s)[0] < 3:
            group = group + l_seq[s]
    l_head[me_g] = group
    for step in range(1, nh):
        send(l_head.at[me_g], l_head.at[me_g], l_send.at[1], l_recv.at[1], me_s, lax.rem(me_g + step, nh))
    await_bytes(grads, g_recv)
    await_bytes(l_head.at[pl.ds(0, nh - 1)], l_recv.at[1])
    total = l_head[0]
    for g in range(1, nh):
        total = total + l_head[g]
    loss[0] = jnp.sum(total) * (0.125 / (LOG2E * 3.0 * rel_all * tokens))

    await_bytes(teacher.at[:, pl.ds(0, rows - sub), :], p1_send)

    @pl.when(active)
    def _():
        await_bytes(back.at[pl.ds(0, (3 * rels - 1) * rows), :], s_send)
        await_bytes(back.at[pl.ds(0, (ns - 1) * rows), :], g_send)
        await_bytes(t_all.at[pl.ds(0, (3 * rel_all - 1) * sub), :], p2_send)
        await_bytes(l_seq.at[pl.ds(0, ns - 1)], l_send.at[0])

    @pl.when(jnp.logical_not(active))
    def _():
        await_bytes(back.at[pl.ds(0, 3 * rels * rows), :], s_send)
        await_bytes(t_all.at[pl.ds(0, 3 * rel_all * sub), :], p2_send)

    await_bytes(l_head.at[pl.ds(0, nh - 1)], l_send.at[1])


def solution(mesh):
    ns = mesh.shape["seq"]
    nh = mesh.shape["head"]

    def body(teacher, student, table):
        rows, _, width = teacher.shape
        swidth = student.shape[2]
        sub = rows // nh
        rel_all = swidth // HD * nh
        tokens = rows * ns
        blocks = tokens // BLK
        tiles = blocks * (blocks + 1) // 2
        dma = pltpu.SemaphoreType.DMA
        loss, grads = pl.pallas_call(
            functools.partial(kernel, ns, nh),
            out_shape=(
                jax.ShapeDtypeStruct((1,), F32),
                jax.ShapeDtypeStruct((3, rows, swidth), BF16),
            ),
            in_specs=[
                pl.BlockSpec(memory_space=pltpu.HBM),
                pl.BlockSpec(memory_space=pltpu.HBM),
                pl.BlockSpec(memory_space=pltpu.HBM),
            ],
            out_specs=(
                pl.BlockSpec(memory_space=pltpu.SMEM),
                pl.BlockSpec(memory_space=pl.ANY),
            ),
            scratch_shapes=[pltpu.SMEM(table.shape, jnp.int32)]
            + [pltpu.VMEM((nh, sub, width), BF16)] * 3
            + [pltpu.VMEM((width // HD * nh, sub, HD), BF16)] * 3
            + [pltpu.VMEM((rel_all, sub, GRP * HD), BF16)] * 3
            + [
                pltpu.VMEM((tokens, GRP * HD), BF16),
                pltpu.VMEM((tokens, HD), BF16),
                pltpu.VMEM((HD, tokens), BF16),
                pltpu.VMEM((tiles, BLK, BLK), F32),
                pltpu.VMEM((tiles, BLK, BLK), F32),
                pltpu.VMEM((tiles, BLK, BLK), F32),
                pltpu.VMEM((tiles, BLK // CH, 8, BLK), F32),
                pltpu.VMEM((tiles, BLK // CH, 8, BLK), F32),
                pltpu.VMEM((blocks, 8, BLK), F32),
                pltpu.VMEM((blocks, 8, BLK), F32),
                pltpu.VMEM((HD, tokens), F32),
                pltpu.VMEM((tokens, HD), BF16),
                pltpu.VMEM((8, HD), F32),
                pltpu.VMEM((ns, 8, HD), F32),
                pltpu.VMEM((nh, 8, HD), F32),
                dma, dma, dma((3,)), dma, dma, dma, dma((blocks // 2,)), dma, dma, dma((2,)), dma((2,)),
                pltpu.SemaphoreType.REGULAR,
                pltpu.VMEM((3, rows, width), BF16),
                pltpu.VMEM((3, rows, swidth), BF16),
                dma((2,)),
            ],
            compiler_params=pltpu.CompilerParams(
                has_side_effects=True, collective_id=0, vmem_limit_bytes=48 * 1024 * 1024
            ),
            cost_estimate=pl.CostEstimate(
                flops=tokens * tokens * 1280, bytes_accessed=4 * 1024 * 1024,
                transcendentals=tokens * tokens,
            ),
            name="relations",
        )(*[pltpu.with_memory_space_constraint(x, pltpu.HBM) for x in (table, jnp.transpose(teacher, (1, 0, 2)), jnp.transpose(student, (1, 0, 2)))])
        return loss.reshape(()), jnp.transpose(grads, (1, 0, 2))

    return jax.shard_map(
        body,
        mesh=mesh,
        in_specs=(P("seq", None, "head"), P("seq", None, "head"), P()),
        out_specs=(P(), P("seq", None, "head")),
        check_vma=False,
    )
```

```python
import functools
import math

import jax
import jax.numpy as jnp
from jax import lax
from jax.experimental import pallas as pl
from jax.experimental.pallas import tpu as pltpu
from jax.sharding import PartitionSpec as P

HD = 128
GRP = 2
BLK = 256
CH = 256
NEG = -1e30
MESH = pl.DeviceIdType.MESH
SEQ_FAR = [(z, k) for z in (2, 1, 3, 0) for k in (2, 3, 1, 0) if z or k]
FAR_FIRST = [(2, 1), (1, 1), (3, 1), (2, 0), (0, 1), (1, 0), (3, 0)]
F32 = jnp.float32
BF16 = jnp.bfloat16
LOG2E = math.log2(math.e)


def owner_seq(p, rl):
    return 4 * rl + lax.rem(p + rl + 1, 4)


def owner_of_static(s):
    rl = s // 4
    p = (s % 4 - rl - 1) % 4
    return p, rl


def await_bytes(ref, sem):
    pltpu.make_async_copy(ref, ref, sem).wait()


def dot_t(a, b):
    return lax.dot_general(a, b, (((1,), (1,)), ((), ())), preferred_element_type=F32)


def kernel(
    ns, nh, table_hbm, teacher, student, loss, grads, table,
    got0, got1, got2, flat0, flat1, flat2, stage0, stage1, stage2,
    t_all, s_all, s_turn, log_s, w_s, w_t, top_s, top_t, lse_s, lse_t, rows_turned, back,
    l_mine, l_seq, l_head,
    tab_sem, p1_send, p1_recv, s_send, s_recv, p2_send, t_recv, g_send, g_recv, l_send, l_recv, all_in, t_near, s_near, pre_sem,
):
    rows = teacher.shape[1]
    width = teacher.shape[2]
    slots = width // HD
    sub = rows // nh
    rels = student.shape[2] // HD
    rel_all = rels * nh
    tokens = rows * ns
    wide = tokens // (2 * BLK)
    per_blk = 2 * BLK // rows
    me_s = lax.axis_index("seq")
    me_g = lax.axis_index("head")
    my_rl = me_s // 4
    my_p = lax.rem(lax.rem(me_s, 4) - my_rl + 7, 4)
    active = my_p < 3
    got = (got0, got1, got2)
    flat = (flat0, flat1, flat2)
    stage = (stage0, stage1, stage2)

    def send(src, dst, ssem, rsem, s, g):
        pltpu.make_async_remote_copy(
            src_ref=src, dst_ref=dst, send_sem=ssem, recv_sem=rsem,
            device_id=(s, g), device_id_type=MESH,
        ).start()

    barrier = pltpu.get_barrier_semaphore()

    def greet(sem, along_seq):
        for step in range(1, ns if along_seq else nh):
            if along_seq:
                dz, dk = SEQ_FAR[step - 1]
                to = (lax.rem(me_s // 4 + dz, 4) * 4 + lax.rem(me_s + dk, 4), me_g)
            else:
                dy, dx = FAR_FIRST[step - 1]
                to = (me_s, lax.rem(me_g // 2 + dy, nh // 2) * 2 + lax.rem(me_g + dx, 2))
            pl.semaphore_signal(sem, inc=1, device_id=to, device_id_type=MESH)

    greet(barrier, False)
    greet(barrier, True)
    table_copy = pltpu.make_async_copy(table_hbm, table, tab_sem)
    table_copy.start()
    pre_t = pltpu.make_async_copy(teacher, t_near, pre_sem.at[0])
    pre_s = pltpu.make_async_copy(student, s_near, pre_sem.at[1])
    pre_t.start()
    pre_s.start()
    pl.semaphore_wait(barrier, ns + nh - 2)
    pre_t.wait()
    teacher, student = t_near, s_near

    def student_out(i, c):
        q = lax.rem(i + me_s, 3 * rels)
        p = q // rels
        rl = lax.rem(q, rels)
        s = owner_seq(p, rl)
        src = student.at[p, :, pl.ds(pl.multiple_of(rl * HD, HD), HD)]
        dst = s_all.at[pl.ds(pl.multiple_of(me_s * rows, rows), rows), :]

        @pl.when(s != me_s)
        def _():
            send(src, dst, s_send, s_recv, s, me_g)

        @pl.when(s == me_s)
        def _():
            pltpu.make_async_copy(src, dst, s_recv).start()

        return c

    for p in range(3):
        for step in range(1, nh):
            dy, dx = FAR_FIRST[step - 1]
            g = lax.rem(me_g // 2 + dy, nh // 2) * 2 + lax.rem(me_g + dx, 2)
            send(
                teacher.at[p, pl.ds(g * sub, sub), :], got[p].at[me_g],
                p1_send, p1_recv.at[p], me_s, g,
            )
            if p == 2:
                if step == 1:
                    pre_s.wait()
                student_out(step - 1, 0)
        pltpu.make_async_copy(
            teacher.at[p, pl.ds(me_g * sub, sub), :], got[p].at[me_g], p1_recv.at[p]
        ).start()

    greet(all_in, False)

    lax.fori_loop(nh - 1, 3 * rels, student_out, 0)
    table_copy.wait()
    pl.semaphore_wait(all_in, nh - 1)

    for p in range(3):
        await_bytes(got[p], p1_recv.at[p])
        for h in range(slots * nh):
            lane = h % slots * HD
            flat[p][h] = got[p][h // slots, :, lane : lane + HD]

        def relation_out(i, c):
            r = lax.rem(i + 2 * me_s + rels * me_g, rel_all)
            for k in range(GRP):
                stage[p][r, :, k * HD : (k + 1) * HD] = flat[p][table[GRP * r + k]]
            g = r // rels
            s = owner_seq(p, lax.rem(r, rels))
            src = stage[p].at[r]
            dst = t_all.at[pl.ds(pl.multiple_of(me_s * rows + me_g * sub, sub), sub), :]
            here = jnp.logical_and(s == me_s, g == me_g)

            @pl.when(jnp.logical_not(here))
            def _():
                send(src, dst, p2_send, t_recv.at[me_s // per_blk], s, g)

            @pl.when(here)
            def _():
                pltpu.make_async_copy(src, dst, t_recv.at[me_s // per_blk]).start()

            return c

        lax.fori_loop(0, rel_all, relation_out, 0)

    scale_t = LOG2E / math.sqrt(GRP * HD)
    scale_s = LOG2E / math.sqrt(HD)
    key_row = lax.broadcasted_iota(jnp.int32, (BLK, BLK), 0)
    query_col = lax.broadcasted_iota(jnp.int32, (BLK, BLK), 1)
    deep = (CH // 8, 8, BLK)

    def at_block(b):
        return pl.ds(pl.multiple_of(b * BLK, BLK), BLK)

    def tile_of(kb, qb):
        return qb * (qb + 1) // 2 + kb

    def logits(feats, kb, query, scale, diagonal):
        out = dot_t(feats[at_block(kb), :], query) * scale
        if diagonal:
            out = jnp.where(key_row <= query_col, out, NEG)
        return [out[c * CH : (c + 1) * CH].reshape(deep) for c in range(BLK // CH)]

    def student_tile(kb, qb, query, state, diagonal):
        top, total = state
        t = tile_of(kb, qb)
        for c, logit in enumerate(logits(s_all, kb, query, scale_s, diagonal)):
            new = jnp.maximum(top, jnp.max(logit, axis=0))
            weight = jnp.exp2(logit - new)
            log_s[t, c * CH : (c + 1) * CH, :] = logit.reshape(CH, BLK)
            w_s[t, c * CH : (c + 1) * CH, :] = weight.reshape(CH, BLK)
            top_s[t, c] = new
            total = total * jnp.exp2(top - new) + jnp.sum(weight, axis=0)
            top = new
        return top, total

    def teacher_tile(kb, qb, query, state, diagonal):
        top, total, cross = state
        t = tile_of(kb, qb)
        for c, logit in enumerate(logits(t_all, kb, query, scale_t, diagonal)):
            new = jnp.maximum(top, jnp.max(logit, axis=0))
            weight = jnp.exp2(logit - new)
            w_t[t, c * CH : (c + 1) * CH, :] = weight.reshape(CH, BLK)
            top_t[t, c] = new
            again = jnp.exp2(top - new)
            gap = logit - log_s[t, c * CH : (c + 1) * CH, :].reshape(deep)
            total = total * again + jnp.sum(weight, axis=0)
            cross = cross * again + jnp.sum(weight * gap, axis=0)
            top = new
        return top, total, cross

    def sweep(tile, feats, wq, fresh):
        qa, qb = 2 * wq, 2 * wq + 1
        query_a, query_b = feats[at_block(qa), :], feats[at_block(qb), :]

        def full(i, c):
            state_a, state_b = c
            for kb in (2 * i, 2 * i + 1):
                state_a = tile(kb, qa, query_a, state_a, False)
                state_b = tile(kb, qb, query_b, state_b, False)
            return state_a, state_b

        state_a, state_b = fresh, fresh
        for i in range(wq):
            state_a, state_b = full(i, (state_a, state_b))
        state_a = tile(qa, qa, query_a, state_a, True)
        state_b = tile(qa, qb, query_b, state_b, False)
        state_b = tile(qb, qb, query_b, state_b, True)
        return (qa, state_a), (qb, state_b)

    def loop(n, f, init):
        for i in range(n):
            init = f(i, init)
        return init

    low = jnp.full((8, BLK), NEG, F32)
    zero = jnp.zeros((8, BLK), F32)

    @pl.when(active)
    def _():
        await_bytes(s_all, s_recv)

        def turn(b, c):
            s_turn[:, at_block(b)] = s_all[at_block(b), :].T
            return c

        lax.fori_loop(0, 2 * wide, turn, 0)

        def student_block(wq, c):
            for q, (top, total) in sweep(student_tile, s_all, wq, (low, zero)):
                peak = jnp.max(top, axis=0, keepdims=True)
                total = jnp.sum(total * jnp.exp2(top - peak), axis=0, keepdims=True)
                lse_s[q] = jnp.broadcast_to(peak + jnp.log2(total), (8, BLK))
            return c

        loop(wide, student_block, 0)

        def teacher_block(wq, loss_row):
            await_bytes(t_all.at[pl.ds(2 * wq * BLK, 2 * BLK), :], t_recv.at[wq])
            for q, (top, total, cross) in sweep(teacher_tile, t_all, wq, (low, zero, zero)):
                peak = jnp.max(top, axis=0, keepdims=True)
                again = jnp.exp2(top - peak)
                total = jnp.sum(total * again, axis=0, keepdims=True)
                cross = jnp.sum(cross * again, axis=0, keepdims=True)
                lse = jnp.broadcast_to(peak + jnp.log2(total), (8, BLK))
                lse_t[q] = lse
                loss_row = loss_row + (cross / total - lse + lse_s[q])
            return loss_row

        loss_row = loop(wide, teacher_block, zero)
        mine = loss_row[:, :HD] + loss_row[:, HD:]
        l_mine[...] = mine
        l_seq[me_s] = mine

        def loss_out(i, c):
            s = 4 * (i // 4) + lax.rem(me_s + i, 4)

            @pl.when(s != me_s)
            def _():
                send(l_mine, l_seq.at[me_s], l_send.at[0], l_recv.at[0], s, me_g)

            return c

        lax.fori_loop(0, ns, loss_out, 0)

        def diff(kb, q):
            t = tile_of(kb, q)
            parts = []
            for c in range(BLK // CH):
                ours = w_s[t, c * CH : (c + 1) * CH, :].reshape(deep) * jnp.exp2(top_s[t, c] - lse_s[q])
                theirs = w_t[t, c * CH : (c + 1) * CH, :].reshape(deep) * jnp.exp2(top_t[t, c] - lse_t[q])
                parts.append((ours - theirs).reshape(CH, BLK).astype(BF16))
            return jnp.concatenate(parts, axis=0)

        for kb in range(2 * wide):
            keys_turned = s_turn[:, at_block(kb)]
            col = jnp.zeros((BLK, HD), F32)
            for q in range(kb, 2 * wide):
                d = diff(kb, q)
                col = col + jnp.dot(d, s_all[at_block(q), :], preferred_element_type=F32)
                row = jnp.dot(keys_turned, d, preferred_element_type=F32)
                if kb > 0:
                    row = row + rows_turned[:, at_block(q)]
                if q > kb:
                    rows_turned[:, at_block(q)] = row
                else:
                    last = row
            back[at_block(kb), :] = ((col + last.T) * (1.0 / math.sqrt(HD))).astype(BF16)
            for j in range(BLK // rows):
                s = kb * (BLK // rows) + j
                src = back.at[pl.ds(s * rows, rows), :]
                dst = grads.at[my_p, :, pl.ds(pl.multiple_of(my_rl * HD, HD), HD)]

                @pl.when(s != me_s)
                def _():
                    send(src, dst, g_send, g_recv, s, me_g)

                @pl.when(s == me_s)
                def _():
                    pltpu.make_async_copy(src, dst, g_recv).start()

        await_bytes(l_seq.at[pl.ds(0, 3 * rels - 1)], l_recv.at[0])

    @pl.when(jnp.logical_not(active))
    def _():
        await_bytes(l_seq.at[pl.ds(0, 3 * rels)], l_recv.at[0])

    group = jnp.zeros((8, HD), F32)
    for s in range(ns):
        if owner_of_static(s)[0] < 3:
            group = group + l_seq[s]
    l_head[me_g] = group
    for step in range(1, nh):
        dy, dx = FAR_FIRST[step - 1]
        g = lax.rem(me_g // 2 + dy, nh // 2) * 2 + lax.rem(me_g + dx, 2)
        send(l_head.at[me_g], l_head.at[me_g], l_send.at[1], l_recv.at[1], me_s, g)
    await_bytes(grads, g_recv)
    await_bytes(l_head.at[pl.ds(0, nh - 1)], l_recv.at[1])
    total = l_head[0]
    for g in range(1, nh):
        total = total + l_head[g]
    loss[0] = jnp.sum(total) * (0.125 / (LOG2E * 3.0 * rel_all * tokens))

    await_bytes(teacher.at[:, pl.ds(0, rows - sub), :], p1_send)

    @pl.when(active)
    def _():
        await_bytes(back.at[pl.ds(0, (3 * rels - 1) * rows), :], s_send)
        await_bytes(back.at[pl.ds(0, (ns - 1) * rows), :], g_send)
        await_bytes(t_all.at[pl.ds(0, (3 * rel_all - 1) * sub), :], p2_send)
        await_bytes(l_seq.at[pl.ds(0, ns - 1)], l_send.at[0])

    @pl.when(jnp.logical_not(active))
    def _():
        await_bytes(back.at[pl.ds(0, 3 * rels * rows), :], s_send)
        await_bytes(t_all.at[pl.ds(0, 3 * rel_all * sub), :], p2_send)

    await_bytes(l_head.at[pl.ds(0, nh - 1)], l_send.at[1])


def solution(mesh):
    ns = mesh.shape["seq"]
    nh = mesh.shape["head"]

    def body(teacher, student, table):
        rows, _, width = teacher.shape
        swidth = student.shape[2]
        sub = rows // nh
        rel_all = swidth // HD * nh
        tokens = rows * ns
        blocks = tokens // BLK
        tiles = blocks * (blocks + 1) // 2
        dma = pltpu.SemaphoreType.DMA
        loss, grads = pl.pallas_call(
            functools.partial(kernel, ns, nh),
            out_shape=(
                jax.ShapeDtypeStruct((1,), F32),
                jax.ShapeDtypeStruct((3, rows, swidth), BF16),
            ),
            in_specs=[
                pl.BlockSpec(memory_space=pltpu.HBM),
                pl.BlockSpec(memory_space=pltpu.HBM),
                pl.BlockSpec(memory_space=pltpu.HBM),
            ],
            out_specs=(
                pl.BlockSpec(memory_space=pltpu.SMEM),
                pl.BlockSpec(memory_space=pl.ANY),
            ),
            scratch_shapes=[pltpu.SMEM(table.shape, jnp.int32)]
            + [pltpu.VMEM((nh, sub, width), BF16)] * 3
            + [pltpu.VMEM((width // HD * nh, sub, HD), BF16)] * 3
            + [pltpu.VMEM((rel_all, sub, GRP * HD), BF16)] * 3
            + [
                pltpu.VMEM((tokens, GRP * HD), BF16),
                pltpu.VMEM((tokens, HD), BF16),
                pltpu.VMEM((HD, tokens), BF16),
                pltpu.VMEM((tiles, BLK, BLK), F32),
                pltpu.VMEM((tiles, BLK, BLK), F32),
                pltpu.VMEM((tiles, BLK, BLK), F32),
                pltpu.VMEM((tiles, BLK // CH, 8, BLK), F32),
                pltpu.VMEM((tiles, BLK // CH, 8, BLK), F32),
                pltpu.VMEM((blocks, 8, BLK), F32),
                pltpu.VMEM((blocks, 8, BLK), F32),
                pltpu.VMEM((HD, tokens), F32),
                pltpu.VMEM((tokens, HD), BF16),
                pltpu.VMEM((8, HD), F32),
                pltpu.VMEM((ns, 8, HD), F32),
                pltpu.VMEM((nh, 8, HD), F32),
                dma, dma, dma((3,)), dma, dma, dma, dma((blocks // 2,)), dma, dma, dma((2,)), dma((2,)),
                pltpu.SemaphoreType.REGULAR,
                pltpu.VMEM((3, rows, width), BF16),
                pltpu.VMEM((3, rows, swidth), BF16),
                dma((2,)),
            ],
            compiler_params=pltpu.CompilerParams(
                has_side_effects=True, collective_id=0, vmem_limit_bytes=48 * 1024 * 1024
            ),
            cost_estimate=pl.CostEstimate(
                flops=tokens * tokens * 1280, bytes_accessed=4 * 1024 * 1024,
                transcendentals=tokens * tokens,
            ),
            name="relations",
        )(*[pltpu.with_memory_space_constraint(x, pltpu.HBM) for x in (table, jnp.transpose(teacher, (1, 0, 2)), jnp.transpose(student, (1, 0, 2)))])
        return loss.reshape(()), jnp.transpose(grads, (1, 0, 2))

    return jax.shard_map(
        body,
        mesh=mesh,
        in_specs=(P("seq", None, "head"), P("seq", None, "head"), P()),
        out_specs=(P(), P("seq", None, "head")),
        check_vma=False,
    )
```

```python
import functools
import math

import jax
import jax.numpy as jnp
from jax import lax
from jax.experimental import pallas as pl
from jax.experimental.pallas import tpu as pltpu
from jax.sharding import PartitionSpec as P

HD = 128
GRP = 2
BLK = 256
CH = 256
NEG = -1e30
MESH = pl.DeviceIdType.MESH
FAR_FIRST = [(2, 1), (1, 1), (3, 1), (2, 0), (0, 1), (1, 0), (3, 0)]
F32 = jnp.float32
BF16 = jnp.bfloat16
LOG2E = math.log2(math.e)


def owner_seq(p, rl):
    return 4 * rl + lax.rem(p + rl + 1, 4)


def owner_of_static(s):
    rl = s // 4
    p = (s % 4 - rl - 1) % 4
    return p, rl


def await_bytes(ref, sem):
    pltpu.make_async_copy(ref, ref, sem).wait()


def dot_t(a, b):
    return lax.dot_general(a, b, (((1,), (1,)), ((), ())), preferred_element_type=F32)


def kernel(
    ns, nh, table_hbm, teacher, student, loss, grads, table,
    got0, got1, got2, flat0, flat1, flat2, stage0, stage1, stage2,
    t_all, s_all, s_turn, log_s, w_s, w_t, top_s, top_t, lse_s, lse_t, rows_turned, back,
    l_mine, l_seq, l_head,
    tab_sem, p1_send, p1_recv, s_send, s_recv, p2_send, t_recv, g_send, g_recv, l_send, l_recv, all_in, t_near, s_near, pre_sem,
):
    rows = teacher.shape[1]
    width = teacher.shape[2]
    slots = width // HD
    sub = rows // nh
    rels = student.shape[2] // HD
    rel_all = rels * nh
    tokens = rows * ns
    wide = tokens // (2 * BLK)
    per_blk = 2 * BLK // rows
    me_s = lax.axis_index("seq")
    me_g = lax.axis_index("head")
    my_rl = me_s // 4
    my_p = lax.rem(lax.rem(me_s, 4) - my_rl + 7, 4)
    active = my_p < 3
    got = (got0, got1, got2)
    flat = (flat0, flat1, flat2)
    stage = (stage0, stage1, stage2)

    def send(src, dst, ssem, rsem, s, g):
        pltpu.make_async_remote_copy(
            src_ref=src, dst_ref=dst, send_sem=ssem, recv_sem=rsem,
            device_id=(s, g), device_id_type=MESH,
        ).start()

    barrier = pltpu.get_barrier_semaphore()

    def greet(sem, along_seq):
        def one(i, c):
            if along_seq:
                to = (lax.rem(me_s + i, ns), me_g)
            else:
                to = (me_s, lax.rem(me_g + i, nh))
            pl.semaphore_signal(sem, inc=1, device_id=to, device_id_type=MESH)
            return c

        lax.fori_loop(1, ns if along_seq else nh, one, 0)

    greet(barrier, False)
    greet(barrier, True)
    table_copy = pltpu.make_async_copy(table_hbm, table, tab_sem)
    table_copy.start()
    pre_t = pltpu.make_async_copy(teacher, t_near, pre_sem.at[0])
    pre_s = pltpu.make_async_copy(student, s_near, pre_sem.at[1])
    pre_t.start()
    pre_s.start()
    pl.semaphore_wait(barrier, ns + nh - 2)
    pre_t.wait()
    pre_s.wait()
    teacher, student = t_near, s_near

    for p in range(3):
        for step in range(1, nh):
            dy, dx = FAR_FIRST[step - 1] if nh == 8 else (step // 2, step % 2)
            g = lax.rem(me_g // 2 + dy, nh // 2) * 2 + lax.rem(me_g + dx, 2)
            send(
                teacher.at[p, pl.ds(g * sub, sub), :], got[p].at[me_g],
                p1_send, p1_recv.at[p], me_s, g,
            )
        pltpu.make_async_copy(
            teacher.at[p, pl.ds(me_g * sub, sub), :], got[p].at[me_g], p1_recv.at[p]
        ).start()

    greet(all_in, False)

    def student_out(i, c):
        q = lax.rem(i + me_s, 3 * rels)
        p = q // rels
        rl = lax.rem(q, rels)
        s = owner_seq(p, rl)
        src = student.at[p, :, pl.ds(pl.multiple_of(rl * HD, HD), HD)]
        dst = s_all.at[pl.ds(pl.multiple_of(me_s * rows, rows), rows), :]

        @pl.when(s != me_s)
        def _():
            send(src, dst, s_send, s_recv, s, me_g)

        @pl.when(s == me_s)
        def _():
            pltpu.make_async_copy(src, dst, s_recv).start()

        return c

    lax.fori_loop(0, 3 * rels, student_out, 0)
    table_copy.wait()
    pl.semaphore_wait(all_in, nh - 1)

    for p in range(3):
        await_bytes(got[p], p1_recv.at[p])
        for h in range(slots * nh):
            lane = h % slots * HD
            flat[p][h] = got[p][h // slots, :, lane : lane + HD]

        def relation_out(i, c):
            r = lax.rem(i + 2 * me_s + rels * me_g, rel_all)
            for k in range(GRP):
                stage[p][r, :, k * HD : (k + 1) * HD] = flat[p][table[GRP * r + k]]
            g = r // rels
            s = owner_seq(p, lax.rem(r, rels))
            src = stage[p].at[r]
            dst = t_all.at[pl.ds(pl.multiple_of(me_s * rows + me_g * sub, sub), sub), :]
            here = jnp.logical_and(s == me_s, g == me_g)

            @pl.when(jnp.logical_not(here))
            def _():
                send(src, dst, p2_send, t_recv.at[me_s // per_blk], s, g)

            @pl.when(here)
            def _():
                pltpu.make_async_copy(src, dst, t_recv.at[me_s // per_blk]).start()

            return c

        lax.fori_loop(0, rel_all, relation_out, 0)

    scale_t = LOG2E / math.sqrt(GRP * HD)
    scale_s = LOG2E / math.sqrt(HD)
    key_row = lax.broadcasted_iota(jnp.int32, (BLK, BLK), 0)
    query_col = lax.broadcasted_iota(jnp.int32, (BLK, BLK), 1)
    deep = (CH // 8, 8, BLK)

    def at_block(b):
        return pl.ds(pl.multiple_of(b * BLK, BLK), BLK)

    def tile_of(kb, qb):
        return qb * (qb + 1) // 2 + kb

    def logits(feats, kb, query, scale, diagonal):
        out = dot_t(feats[at_block(kb), :], query) * scale
        if diagonal:
            out = jnp.where(key_row <= query_col, out, NEG)
        return [out[c * CH : (c + 1) * CH].reshape(deep) for c in range(BLK // CH)]

    def student_tile(kb, qb, query, state, diagonal):
        top, total = state
        t = tile_of(kb, qb)
        for c, logit in enumerate(logits(s_all, kb, query, scale_s, diagonal)):
            new = jnp.maximum(top, jnp.max(logit, axis=0))
            weight = jnp.exp2(logit - new)
            log_s[t, c * CH : (c + 1) * CH, :] = logit.reshape(CH, BLK)
            w_s[t, c * CH : (c + 1) * CH, :] = weight.reshape(CH, BLK)
            top_s[t, c] = new
            total = total * jnp.exp2(top - new) + jnp.sum(weight, axis=0)
            top = new
        return top, total

    def teacher_tile(kb, qb, query, state, diagonal):
        top, total, cross = state
        t = tile_of(kb, qb)
        for c, logit in enumerate(logits(t_all, kb, query, scale_t, diagonal)):
            new = jnp.maximum(top, jnp.max(logit, axis=0))
            weight = jnp.exp2(logit - new)
            w_t[t, c * CH : (c + 1) * CH, :] = weight.reshape(CH, BLK)
            top_t[t, c] = new
            again = jnp.exp2(top - new)
            gap = logit - log_s[t, c * CH : (c + 1) * CH, :].reshape(deep)
            total = total * again + jnp.sum(weight, axis=0)
            cross = cross * again + jnp.sum(weight * gap, axis=0)
            top = new
        return top, total, cross

    def sweep(tile, feats, wq, fresh):
        qa, qb = 2 * wq, 2 * wq + 1
        query_a, query_b = feats[at_block(qa), :], feats[at_block(qb), :]

        def full(i, c):
            state_a, state_b = c
            for kb in (2 * i, 2 * i + 1):
                state_a = tile(kb, qa, query_a, state_a, False)
                state_b = tile(kb, qb, query_b, state_b, False)
            return state_a, state_b

        state_a, state_b = fresh, fresh
        for i in range(wq):
            state_a, state_b = full(i, (state_a, state_b))
        state_a = tile(qa, qa, query_a, state_a, True)
        state_b = tile(qa, qb, query_b, state_b, False)
        state_b = tile(qb, qb, query_b, state_b, True)
        return (qa, state_a), (qb, state_b)

    def loop(n, f, init):
        for i in range(n):
            init = f(i, init)
        return init

    low = jnp.full((8, BLK), NEG, F32)
    zero = jnp.zeros((8, BLK), F32)

    def give_back(kb):
        for j in range(BLK // rows):
            s = kb * (BLK // rows) + j
            src = back.at[pl.ds(s * rows, rows), :]
            dst = grads.at[my_p, :, pl.ds(pl.multiple_of(my_rl * HD, HD), HD)]

            @pl.when(s != me_s)
            def _():
                send(src, dst, g_send, g_recv, s, me_g)

            @pl.when(s == me_s)
            def _():
                pltpu.make_async_copy(src, dst, g_recv).start()

    @pl.when(active)
    def _():
        await_bytes(s_all, s_recv)

        def turn(b, c):
            s_turn[:, at_block(b)] = s_all[at_block(b), :].T
            return c

        lax.fori_loop(0, 2 * wide, turn, 0)

        def student_block(wq, c):
            for q, (top, total) in sweep(student_tile, s_all, wq, (low, zero)):
                peak = jnp.max(top, axis=0, keepdims=True)
                total = jnp.sum(total * jnp.exp2(top - peak), axis=0, keepdims=True)
                lse_s[q] = jnp.broadcast_to(peak + jnp.log2(total), (8, BLK))
            return c

        loop(wide, student_block, 0)

        def teacher_block(wq, loss_row):
            await_bytes(t_all.at[pl.ds(2 * wq * BLK, 2 * BLK), :], t_recv.at[wq])
            for q, (top, total, cross) in sweep(teacher_tile, t_all, wq, (low, zero, zero)):
                peak = jnp.max(top, axis=0, keepdims=True)
                again = jnp.exp2(top - peak)
                total = jnp.sum(total * again, axis=0, keepdims=True)
                cross = jnp.sum(cross * again, axis=0, keepdims=True)
                lse = jnp.broadcast_to(peak + jnp.log2(total), (8, BLK))
                lse_t[q] = lse
                loss_row = loss_row + (cross / total - lse + lse_s[q])
            return loss_row

        loss_row = loop(wide, teacher_block, zero)
        mine = loss_row[:, :HD] + loss_row[:, HD:]
        l_mine[...] = mine
        l_seq[me_s] = mine

        def loss_out(i, c):
            s = 4 * (i // 4) + lax.rem(me_s + i, 4)

            @pl.when(s != me_s)
            def _():
                send(l_mine, l_seq.at[me_s], l_send.at[0], l_recv.at[0], s, me_g)

            return c

        lax.fori_loop(0, ns, loss_out, 0)

        def diff(kb, q):
            t = tile_of(kb, q)
            parts = []
            for c in range(BLK // CH):
                ours = w_s[t, c * CH : (c + 1) * CH, :].reshape(deep) * jnp.exp2(top_s[t, c] - lse_s[q])
                theirs = w_t[t, c * CH : (c + 1) * CH, :].reshape(deep) * jnp.exp2(top_t[t, c] - lse_t[q])
                parts.append((ours - theirs).reshape(CH, BLK).astype(BF16))
            return jnp.concatenate(parts, axis=0)

        for kb in range(2 * wide):
            keys_turned = s_turn[:, at_block(kb)]
            col = jnp.zeros((BLK, HD), F32)
            for q in range(kb, 2 * wide):
                d = diff(kb, q)
                col = col + jnp.dot(d, s_all[at_block(q), :], preferred_element_type=F32)
                row = jnp.dot(keys_turned, d, preferred_element_type=F32)
                if kb > 0:
                    row = row + rows_turned[:, at_block(q)]
                if q > kb:
                    rows_turned[:, at_block(q)] = row
                else:
                    last = row
            back[at_block(kb), :] = ((col + last.T) * (1.0 / math.sqrt(HD))).astype(BF16)
            if kb < 2 * wide - 2:
                give_back(kb)

        await_bytes(l_seq.at[pl.ds(0, 3 * rels - 1)], l_recv.at[0])

    @pl.when(jnp.logical_not(active))
    def _():
        await_bytes(l_seq.at[pl.ds(0, 3 * rels)], l_recv.at[0])

    group = jnp.zeros((8, HD), F32)
    for s in range(ns):
        if owner_of_static(s)[0] < 3:
            group = group + l_seq[s]
    l_head[me_g] = group
    for step in range(1, nh):
        send(l_head.at[me_g], l_head.at[me_g], l_send.at[1], l_recv.at[1], me_s, lax.rem(me_g + step, nh))
    @pl.when(active)
    def _():
        for kb in range(2 * wide - 2, 2 * wide):
            give_back(kb)

    await_bytes(grads, g_recv)
    await_bytes(l_head.at[pl.ds(0, nh - 1)], l_recv.at[1])
    total = l_head[0]
    for g in range(1, nh):
        total = total + l_head[g]
    loss[0] = jnp.sum(total) * (0.125 / (LOG2E * 3.0 * rel_all * tokens))

    await_bytes(teacher.at[:, pl.ds(0, rows - sub), :], p1_send)

    @pl.when(active)
    def _():
        await_bytes(back.at[pl.ds(0, (3 * rels - 1) * rows), :], s_send)
        await_bytes(back.at[pl.ds(0, (ns - 1) * rows), :], g_send)
        await_bytes(t_all.at[pl.ds(0, (3 * rel_all - 1) * sub), :], p2_send)
        await_bytes(l_seq.at[pl.ds(0, ns - 1)], l_send.at[0])

    @pl.when(jnp.logical_not(active))
    def _():
        await_bytes(back.at[pl.ds(0, 3 * rels * rows), :], s_send)
        await_bytes(t_all.at[pl.ds(0, 3 * rel_all * sub), :], p2_send)

    await_bytes(l_head.at[pl.ds(0, nh - 1)], l_send.at[1])


def solution(mesh):
    ns = mesh.shape["seq"]
    nh = mesh.shape["head"]

    def body(teacher, student, table):
        rows, _, width = teacher.shape
        swidth = student.shape[2]
        sub = rows // nh
        rel_all = swidth // HD * nh
        tokens = rows * ns
        blocks = tokens // BLK
        tiles = blocks * (blocks + 1) // 2
        dma = pltpu.SemaphoreType.DMA
        loss, grads = pl.pallas_call(
            functools.partial(kernel, ns, nh),
            out_shape=(
                jax.ShapeDtypeStruct((1,), F32),
                jax.ShapeDtypeStruct((3, rows, swidth), BF16),
            ),
            in_specs=[
                pl.BlockSpec(memory_space=pltpu.HBM),
                pl.BlockSpec(memory_space=pltpu.HBM),
                pl.BlockSpec(memory_space=pltpu.HBM),
            ],
            out_specs=(
                pl.BlockSpec(memory_space=pltpu.SMEM),
                pl.BlockSpec(memory_space=pl.ANY),
            ),
            scratch_shapes=[pltpu.SMEM(table.shape, jnp.int32)]
            + [pltpu.VMEM((nh, sub, width), BF16)] * 3
            + [pltpu.VMEM((width // HD * nh, sub, HD), BF16)] * 3
            + [pltpu.VMEM((rel_all, sub, GRP * HD), BF16)] * 3
            + [
                pltpu.VMEM((tokens, GRP * HD), BF16),
                pltpu.VMEM((tokens, HD), BF16),
                pltpu.VMEM((HD, tokens), BF16),
                pltpu.VMEM((tiles, BLK, BLK), F32),
                pltpu.VMEM((tiles, BLK, BLK), F32),
                pltpu.VMEM((tiles, BLK, BLK), F32),
                pltpu.VMEM((tiles, BLK // CH, 8, BLK), F32),
                pltpu.VMEM((tiles, BLK // CH, 8, BLK), F32),
                pltpu.VMEM((blocks, 8, BLK), F32),
                pltpu.VMEM((blocks, 8, BLK), F32),
                pltpu.VMEM((HD, tokens), F32),
                pltpu.VMEM((tokens, HD), BF16),
                pltpu.VMEM((8, HD), F32),
                pltpu.VMEM((ns, 8, HD), F32),
                pltpu.VMEM((nh, 8, HD), F32),
                dma, dma, dma((3,)), dma, dma, dma, dma((blocks // 2,)), dma, dma, dma((2,)), dma((2,)),
                pltpu.SemaphoreType.REGULAR,
                pltpu.VMEM((3, rows, width), BF16),
                pltpu.VMEM((3, rows, swidth), BF16),
                dma((2,)),
            ],
            compiler_params=pltpu.CompilerParams(
                has_side_effects=True, collective_id=0, vmem_limit_bytes=48 * 1024 * 1024
            ),
            cost_estimate=pl.CostEstimate(
                flops=tokens * tokens * 1280, bytes_accessed=4 * 1024 * 1024,
                transcendentals=tokens * tokens,
            ),
            name="relations",
        )(*[pltpu.with_memory_space_constraint(x, pltpu.HBM) for x in (table, jnp.transpose(teacher, (1, 0, 2)), jnp.transpose(student, (1, 0, 2)))])
        return loss.reshape(()), jnp.transpose(grads, (1, 0, 2))

    return jax.shard_map(
        body,
        mesh=mesh,
        in_specs=(P("seq", None, "head"), P("seq", None, "head"), P()),
        out_specs=(P(), P("seq", None, "head")),
        check_vma=False,
    )
```
